256 devices in a mesh: dp: 8 (over z_lo, core), ctx: 32 (over y, x, z_hi).
Axes of the slice: x: 4, y: 4, z: 8 (z_hi: 2, z_lo: 4; z = z_hi * 4 + z_lo), core: 2. Of those that a mesh axis runs over, the one named last changes fastest.
Arguments:
- layer_input: bfloat16 [8, 4096, 16384], P('dp', 'ctx'), may hold values from -6 to 6
- query_rows: bfloat16 [8, 4096, 1024], P('dp', 'ctx'), may hold values from -512 to 512
- key_rows: bfloat16 [8, 4096, 128], P('dp', 'ctx'), may hold values from -5 to 5
- value_rows: bfloat16 [8, 4096, 128], P('dp', 'ctx'), may hold values from -6 to 6
- out_grad: bfloat16 [8, 4096, 1024], P('dp', 'ctx'), may hold values from -6 to 6
- block_order: int32 [64], replicated, may hold values from 0 to 63, each once
- master: float32 [16384, 1280], P(('dp', 'ctx')), may hold values from -3 to 3
- moment_one: float32 [16384, 1280], P(('dp', 'ctx')), may hold values from -6 to 6
- moment_two: float32 [16384, 1280], P(('dp', 'ctx')), may hold values from 0.5 to 20
Outputs:
- new_master: float32 [16384, 1280], P(('dp', 'ctx'))
- new_moment_one: float32 [16384, 1280], P(('dp', 'ctx'))
- new_moment_two: float32 [16384, 1280], P(('dp', 'ctx'))
The draws below stay inside these ranges and needn't reach their ends.
Inputs may be any that keep to these rules, and one draw needn't show every extreme that they name: Stored rows j * 64 to (j + 1) * 64 - 1 of every sequence hold positions block_order[j] * 64 onward, in order; each of the 64 blocks appears once.
All inputs are finite; a program needn't handle non-finite values.
Results may differ from the reference program's by a relative error of at most 0.0048.
Values may be sent and summed in bfloat16 or wider, within the bound.
A program may use at most 64 MiB of HBM per device.

```python
import math
import jax
import jax.numpy as jnp
from jax import lax

D = 16384
HD = 128
GROUP = 8
STEP = 10
BATCH = 8
LENGTH = 4096
HALF = 64
BLOCKS = 64
QW = 1024
QKV = 1280


def draw_common(key):
    keys_all = jnp.clip(jax.random.normal(jax.random.fold_in(key, 11), (BATCH, LENGTH, HD), jnp.float32), -5.0, 5.0)
    query_all = jnp.clip(jax.random.normal(jax.random.fold_in(key, 12), (BATCH, LENGTH, QW), jnp.float32), -5.0, 5.0)
    return (keys_all, query_all)


def draw_key_rows(key, part):
    return draw_common(key)[0].astype(jnp.bfloat16)


def draw_query_rows(key, part):
    return draw_common(key)[1].astype(jnp.bfloat16)


def steps_of(key, dims, pieces, smallest, high):
    def one(position, parts):
        heights = jax.random.uniform(jax.random.fold_in(jax.random.fold_in(key, 6), position), (parts,), jnp.float32, smallest / len(pieces), high / len(pieces))
        return jnp.repeat(jnp.exp(heights), dims[position] // parts).reshape((-1,) + (1,) * (len(dims) - position - 1))

    loudness = one(*pieces[0])
    for cut in pieces[1:]:
        loudness = loudness * one(*cut)
    return loudness


def gaussian(stream_key, shape, deviation, bound, pieces=(), kind=jnp.bfloat16):
    entries = jax.random.normal(stream_key, shape, jnp.float32) * deviation
    if len(pieces) > 0:
        entries = steps_of(stream_key, shape, pieces, -0.22, 0.18) * entries
    return jnp.clip(entries, min=-bound, max=bound).astype(kind)


def setup_inputs(seed: int = 0) -> dict:
    splits = jax.random.split(jax.random.key(seed), 10)
    layer_input = gaussian(splits[0], (BATCH, LENGTH, D), 1.0, 6.0, ((0, 8), (1, 32)))
    query_rows = draw_query_rows(jax.random.fold_in(splits[9], 71), 0)
    key_rows = draw_key_rows(jax.random.fold_in(splits[9], 71), 0)
    value_rows = gaussian(splits[3], (BATCH, LENGTH, HD), 1.0, 6.0, ((0, 8), (1, 32)))
    out_grad = gaussian(splits[4], (BATCH, LENGTH, QW), 1.0, 6.0, ((0, 8), (1, 32)))
    block_order = jax.random.permutation(splits[5], BLOCKS).astype(jnp.int32)
    master = gaussian(splits[6], (D, QKV), 0.5, 3.0, ((0, 256),), jnp.float32)
    moment_one = gaussian(splits[7], (D, QKV), 1.0, 6.0, ((0, 256),), jnp.float32)
    moment_two = jnp.clip(jnp.exp(math.log(20.0) - 3.6888795 * jax.random.uniform(splits[8], (D, QKV), jnp.float32) ** steps_of(splits[8], (D, QKV), ((0, 256),), -0.2, 0.2)), 0.5, 20.0)
    return {"layer_input": layer_input, "query_rows": query_rows, "key_rows": key_rows, "value_rows": value_rows, "out_grad": out_grad, "block_order": block_order, "master": master, "moment_one": moment_one, "moment_two": moment_two}


NEG_FILL = -1e+30
BETA_ONE = 0.9
BETA_TWO = 0.95
EPSILON = 1e-08
LEARN_RATE = 0.01
DECAY = 0.1

def sequence_grads(query_seq, key_seq, value_seq, grad_seq, pos_all):
    score_scale = 1.0 / math.sqrt(HD)
    row_total = LENGTH * GROUP
    rows_q = query_seq.reshape(row_total, HD)
    rows_o = grad_seq.reshape(row_total, HD)
    query_pos = jnp.repeat(pos_all, GROUP)
    blk_rows = math.gcd(row_total, 2048)

    def advance(carried, block_index):
        key_acc, value_acc = carried
        first_row = (block_index * blk_rows).astype(jnp.int32)
        q_blk = lax.dynamic_slice_in_dim(rows_q, first_row, blk_rows, 0)
        o_blk = lax.dynamic_slice_in_dim(rows_o, first_row, blk_rows, 0)
        qpos_blk = lax.dynamic_slice_in_dim(query_pos, first_row, blk_rows, 0)
        scores = jnp.dot(q_blk, key_seq.T, preferred_element_type=jnp.float32) * score_scale
        visible = pos_all[None, :] <= qpos_blk[:, None]
        row_top = lax.optimization_barrier(jnp.max(jnp.where(visible, scores, NEG_FILL), axis=1))
        denom_sum = lax.optimization_barrier(jnp.sum(jnp.where(visible, jnp.exp(scores - row_top[:, None]), 0.0), axis=1))
        log_total = row_top + jnp.log(denom_sum)
        prob_full = jnp.where(visible, jnp.exp(scores - log_total[:, None]), 0.0)
        grad_prob = jnp.dot(o_blk, value_seq.T, preferred_element_type=jnp.float32)
        delta_row = lax.optimization_barrier(jnp.sum(prob_full * grad_prob, axis=1))
        dscore = (prob_full * (grad_prob - delta_row[:, None]) * score_scale).astype(jnp.bfloat16)
        prob_low = prob_full.astype(jnp.bfloat16)
        query_grad = jnp.dot(dscore, key_seq, preferred_element_type=jnp.float32).astype(jnp.bfloat16)
        key_acc = key_acc + jnp.dot(dscore.T, q_blk, preferred_element_type=jnp.float32)
        value_acc = value_acc + jnp.dot(prob_low.T, o_blk, preferred_element_type=jnp.float32)
        return ((key_acc, value_acc), query_grad)
    empty_acc = jnp.zeros((LENGTH, HD), jnp.float32)
    finals, query_grads = lax.scan(advance, (empty_acc, empty_acc), jnp.arange(row_total // blk_rows, dtype=jnp.int32))
    key_acc, value_acc = finals
    return jnp.concatenate([query_grads.reshape(LENGTH, GROUP * HD), key_acc.astype(jnp.bfloat16), value_acc.astype(jnp.bfloat16)], axis=1)

def reference(layer_input, query_rows, key_rows, value_rows, out_grad, block_order, master, moment_one, moment_two):
    pos_all = (block_order[:, None] * HALF + jnp.arange(HALF, dtype=jnp.int32)[None, :]).reshape(LENGTH).astype(jnp.int32)

    def per_sequence(grad_acc, seq_items):
        x_seq, q_seq, k_seq, v_seq, o_seq = seq_items
        grad_cols = sequence_grads(q_seq, k_seq, v_seq, o_seq, pos_all)
        return (grad_acc + jnp.dot(x_seq.T, grad_cols, preferred_element_type=jnp.float32), None)
    grad_full, unused_out = lax.scan(per_sequence, jnp.zeros((D, QKV), jnp.float32), (layer_input, query_rows, key_rows, value_rows, out_grad))
    new_one = BETA_ONE * moment_one + (1.0 - BETA_ONE) * grad_full
    new_two = BETA_TWO * moment_two + (1.0 - BETA_TWO) * grad_full * grad_full
    corr_one = 1.0 - BETA_ONE ** STEP
    corr_two = 1.0 - BETA_TWO ** STEP
    update = new_one / corr_one / (jnp.sqrt(new_two / corr_two) + EPSILON)
    new_master = master - LEARN_RATE * (update + DECAY * master)
    return (new_master, new_one, new_two)
```

```python
import functools
import math

import jax
import jax.numpy as jnp
from jax import lax
from jax.experimental import pallas as pl
from jax.experimental.pallas import tpu as pltpu
from jax.sharding import PartitionSpec as P

STEP = 10
NEG_FILL = -1e30
BETA_ONE = 0.9
BETA_TWO = 0.95
EPSILON = 1e-08
LEARN_RATE = 0.01
DECAY = 0.1

F32 = jnp.float32
BF16 = jnp.bfloat16
MESH = pl.DeviceIdType.MESH
ROW_CONTRACT = (((1,), (1,)), ((), ()))

TOK = 128
HD = 128
HALF = 64
NXY = 16
NCTX = 32
NZ = 8
CHUNK = 256
NCHUNK = 5
KEYS = NCTX * TOK
KT = 512
OWN = 64
ROWS = 1024
SCALE = 1.0 / math.sqrt(HD)


def fused_kernel(
    order_ref,
    x_hbm,
    q_ref,
    k_ref,
    v_ref,
    o_ref,
    grad_ref,
    kv_all,
    k_t,
    x_recv,
    x_t,
    s_scr,
    d_scr,
    dkv_acc,
    dkv_send,
    dkv_recv,
    zkv_send,
    zkv_recv,
    g_all,
    core_send,
    core_recv,
    half_own,
    z_send,
    z_recv,
    kv_ss,
    kv_rs,
    kvz_ss,
    x_ss,
    x_rs,
    g_ss,
    g_rs,
    dkv_ss,
    dkv_rs,
    zkv_ss,
    zkv_rs,
    core_ss,
    core_rs,
    z_ss,
    z_rs,
):
    dp = lax.axis_index("dp")
    ctx = lax.axis_index("ctx")
    core = lax.rem(dp, 2)
    z_lo = dp // 2
    z_hi = lax.rem(ctx, 2)
    plane = ctx // 2
    y = plane // 4
    x = lax.rem(plane, 4)
    z_me = z_hi * 4 + z_lo

    def plane_peer(d):
        return lax.rem(y + d // 4, 4) * 4 + lax.rem(x + lax.rem(d, 4), 4)

    def plane_dev(k):
        return (dp, k * 2 + z_hi)

    def z_peer(d):
        return lax.rem(z_me + d, NZ)

    def z_dev(z):
        return (lax.rem(z, 4) * 2 + core, plane * 2 + z // 4)

    zh_dev = (dp, plane * 2 + (1 - z_hi))
    ctx_other = plane * 2 + (1 - z_hi)
    core_dev = (z_lo * 2 + (1 - core), ctx)

    barrier = pltpu.get_barrier_semaphore()

    @pl.loop(1, NXY)
    def _(d):
        pl.semaphore_signal(barrier, inc=1, device_id=plane_dev(plane_peer(d)), device_id_type=MESH)

    @pl.loop(1, NZ)
    def _(d):
        pl.semaphore_signal(barrier, inc=1, device_id=z_dev(z_peer(d)), device_id_type=MESH)

    pl.semaphore_signal(barrier, inc=1, device_id=core_dev, device_id_type=MESH)

    def rows(first, count):
        return pl.ds(pl.multiple_of(first, count), count)

    my_rows = rows(ctx * TOK, TOK)
    other_rows = rows(ctx_other * TOK, TOK)
    kv_all[my_rows, :HD] = k_ref[...]
    kv_all[my_rows, HD:] = v_ref[...]

    pl.semaphore_wait(barrier, NXY - 1 + NZ - 1 + 1)

    def kv_copy(block_rows, block, d, sems, target):
        return pltpu.make_async_remote_copy(
            src_ref=kv_all.at[block_rows],
            dst_ref=kv_all.at[block_rows],
            send_sem=sems.at[d],
            recv_sem=kv_rs.at[block],
            device_id=target,
            device_id_type=MESH,
        )

    kv_copy(my_rows, ctx, 0, kv_ss, zh_dev).start()

    @pl.loop(1, NXY)
    def _(d):
        kv_copy(my_rows, ctx, d, kv_ss, plane_dev(plane_peer(d))).start()

    kv_copy(other_rows, ctx_other, 0, kv_ss, zh_dev).wait_recv()

    @pl.loop(1, NXY)
    def _(d):
        kv_copy(other_rows, ctx_other, d, kvz_ss, plane_dev(plane_peer(d))).start()

    @pl.loop(1, NXY)
    def _(d):
        k = plane_peer(d)
        for half in range(2):
            block = k * 2 + half
            kv_copy(rows(block * TOK, TOK), block, d, kv_ss, zh_dev).wait_recv()

    def x_copy(k, j, d):
        column = ((j % 4) * 2 + j // 4) * (NCTX * OWN) + k * TOK
        return pltpu.make_async_remote_copy(
            src_ref=x_hbm.at[:, rows(column, TOK)],
            dst_ref=x_recv.at[plane, j],
            send_sem=x_ss.at[d],
            recv_sem=x_rs.at[plane],
            device_id=plane_dev(k),
            device_id_type=MESH,
        )

    def x_own(j):
        column = ((j % 4) * 2 + j // 4) * (NCTX * OWN) + plane * TOK
        return pltpu.make_async_copy(
            x_hbm.at[:, rows(column, TOK)], x_recv.at[plane, j], x_rs.at[plane]
        )

    @pl.loop(1, NXY)
    def _(d):
        for j in range(8):
            x_copy(plane_peer(d), j, d).start()

    for j in range(8):
        x_own(j).start()

    lane = lax.broadcasted_iota(jnp.int32, (1, CHUNK), 1)
    token = lax.rem(lane, TOK)
    query_pos = (
        jnp.where(token < HALF, order_ref[2 * ctx], order_ref[2 * ctx + 1]) * HALF
        + lax.rem(token, HALF)
    )
    sub = lax.broadcasted_iota(jnp.int32, (HALF, CHUNK), 0)

    @pl.loop(0, NCTX)
    def _(b):
        k_t[:, rows(b * TOK, TOK)] = kv_all[rows(b * TOK, TOK), :HD].T

    def g_copy(chunk, k, d):
        piece = g_all.at[chunk, rows(plane * TOK, TOK)]
        return pltpu.make_async_remote_copy(
            src_ref=piece,
            dst_ref=piece,
            send_sem=g_ss.at[chunk, d],
            recv_sem=g_rs.at[chunk, plane],
            device_id=plane_dev(k),
            device_id_type=MESH,
        )

    def send_chunk(chunk):
        @pl.loop(1, NXY)
        def _(d):
            g_copy(chunk, plane_peer(d), d).start()

    def fold(a, op):
        return op(a.reshape(a.shape[0] // 8, 8, a.shape[1]), axis=0)

    for c in range(4):
        heads = (2 * c, 2 * c + 1)
        q_c = jnp.concatenate([q_ref[:, h * HD : (h + 1) * HD] for h in heads], axis=0)
        o_c = jnp.concatenate([o_ref[:, h * HD : (h + 1) * HD] for h in heads], axis=0)

        def scores_tile(t, top):
            first = pl.multiple_of(t * KT, KT)
            s = lax.dot_general(
                kv_all[pl.ds(first, KT), :HD], q_c, ROW_CONTRACT, preferred_element_type=F32
            )
            d_scr[pl.ds(first, KT)] = lax.dot_general(
                kv_all[pl.ds(first, KT), HD:], o_c, ROW_CONTRACT, preferred_element_type=F32
            )
            for b in range(KT // HALF):
                limit = query_pos - order_ref[t * (KT // HALF) + b] * HALF
                part = jnp.where(sub <= limit, s[b * HALF : (b + 1) * HALF], NEG_FILL)
                s_scr[pl.ds(first + b * HALF, HALF)] = part
                top = jnp.maximum(top, fold(part, jnp.max))
            return top

        top = lax.fori_loop(0, KEYS // KT, scores_tile, jnp.full((8, CHUNK), NEG_FILL, F32))
        top = jnp.max(top, axis=0, keepdims=True)

        def weights_tile(t, carried):
            total, inner = carried
            tile = pl.ds(pl.multiple_of(t * KT, KT), KT)
            e = jnp.exp2((s_scr[tile] - top) * (SCALE * math.log2(math.e)))
            s_scr[tile] = e
            return total + fold(e, jnp.sum), inner + fold(e * d_scr[tile], jnp.sum)

        zero = jnp.zeros((8, CHUNK), F32)
        total, inner = lax.fori_loop(0, KEYS // KT, weights_tile, (zero, zero))
        inv = 1.0 / jnp.sum(total, axis=0, keepdims=True)
        delta = jnp.sum(inner, axis=0, keepdims=True) * inv

        def grads_tile(t, dq):
            first = pl.multiple_of(t * KT, KT)
            tile = pl.ds(first, KT)
            p = s_scr[tile] * inv
            ds = (p * (d_scr[tile] - delta) * SCALE).astype(BF16)
            dk = jnp.dot(ds, q_c, preferred_element_type=F32)
            dv = jnp.dot(p.astype(BF16), o_c, preferred_element_type=F32)
            if c == 0:
                dkv_acc[tile, :HD] = dk
                dkv_acc[tile, HD:] = dv
            elif c < 3:
                dkv_acc[tile, :HD] += dk
                dkv_acc[tile, HD:] += dv
            else:
                dkv_send[tile, :HD] = (dkv_acc[tile, :HD] + dk).astype(BF16)
                dkv_send[tile, HD:] = (dkv_acc[tile, HD:] + dv).astype(BF16)
            return dq + jnp.dot(k_t[:, tile], ds, preferred_element_type=F32)

        dq = lax.fori_loop(0, KEYS // KT, grads_tile, jnp.zeros((HD, CHUNK), F32))
        for i in range(2):
            g_all[c, rows(plane * TOK, TOK), i * HD : (i + 1) * HD] = (
                dq[:, i * TOK : (i + 1) * TOK].T.astype(BF16)
            )
        if c == 3:
            @pl.loop(1, NXY)
            def _(d):
                dkv_copy(dkv_send, dkv_recv, dkv_ss, dkv_rs, plane, plane_peer(d), d, plane_dev).start()
        send_chunk(c)

    for j in range(8):
        x_own(j).wait()

    def transpose_slot(k):
        for j in range(8):
            x_t[j * TOK : (j + 1) * TOK, rows(k * TOK, TOK)] = x_recv[k, j].T

    transpose_slot(plane)

    @pl.loop(1, NXY)
    def _(d):
        k = plane_peer(d)
        pltpu.make_async_copy(x_recv.at[k], x_recv.at[k], x_rs.at[k]).wait()
        transpose_slot(k)

    def sum_slot(d, total):
        k = plane_peer(d)
        dkv_copy(dkv_send, dkv_recv, dkv_ss, dkv_rs, k, plane, d, plane_dev).wait_recv()
        return total + dkv_recv[k].astype(F32)

    half_own_kv = lax.fori_loop(
        1, NXY, sum_slot, dkv_send[rows(plane * 2 * TOK, 2 * TOK)].astype(F32)
    )
    zkv_send[...] = half_own_kv.astype(BF16)
    zkv = pltpu.make_async_remote_copy(
        src_ref=zkv_send.at[rows((1 - z_hi) * TOK, TOK)],
        dst_ref=zkv_recv,
        send_sem=zkv_ss,
        recv_sem=zkv_rs,
        device_id=zh_dev,
        device_id_type=MESH,
    )
    zkv.start()
    own_kv = jnp.where(z_hi == 0, half_own_kv[:TOK], half_own_kv[TOK:])
    zkv.wait_recv()
    g_all[4, rows(plane * TOK, TOK)] = (own_kv + zkv_recv[...].astype(F32)).astype(BF16)
    send_chunk(4)

    def z_copy(chunk, z, d):
        return pltpu.make_async_remote_copy(
            src_ref=z_send.at[chunk, z],
            dst_ref=z_recv.at[chunk, z_me],
            send_sem=z_ss.at[chunk, d],
            recv_sem=z_rs.at[chunk, z_me],
            device_id=z_dev(z),
            device_id_type=MESH,
        )

    def z_arrived(chunk, z):
        return pltpu.make_async_remote_copy(
            src_ref=z_send.at[chunk, z],
            dst_ref=z_recv.at[chunk, z],
            send_sem=z_ss.at[chunk, 0],
            recv_sem=z_rs.at[chunk, z],
            device_id=z_dev(z),
            device_id_type=MESH,
        )

    def core_copy(chunk):
        return pltpu.make_async_remote_copy(
            src_ref=core_send.at[chunk],
            dst_ref=core_recv.at[chunk],
            send_sem=core_ss.at[chunk],
            recv_sem=core_rs.at[chunk],
            device_id=core_dev,
            device_id_type=MESH,
        )

    for c in range(NCHUNK):
        @pl.loop(1, NXY)
        def _(d):
            k = plane_peer(d)
            piece = g_all.at[c, rows(k * TOK, TOK)]
            pltpu.make_async_remote_copy(
                src_ref=piece,
                dst_ref=piece,
                send_sem=g_ss.at[c, d],
                recv_sem=g_rs.at[c, k],
                device_id=plane_dev(k),
                device_id_type=MESH,
            ).wait_recv()

        def product(first):
            return jnp.dot(
                x_t[pl.ds(pl.multiple_of(first, 256), 256)], g_all[c], preferred_element_type=F32
            )

        @pl.loop(0, 2)
        def _(i):
            core_send[c, rows(i * 256, 256)] = product((1 - core) * 512 + i * 256)

        core_copy(c).start()

        @pl.loop(0, 2)
        def _(i):
            half_own[c, rows(i * 256, 256)] = product(core * 512 + i * 256)

        core_copy(c).wait_recv()
        for j in range(NZ):
            z = (j % 2) * 4 + j // 2
            part = pl.ds(j * OWN, OWN)
            total = half_own[c, part] + core_recv[c, part]
            half_own[c, part] = total
            z_send[c, z] = total.astype(BF16)

        @pl.loop(1, NZ)
        def _(d):
            z_copy(c, z_peer(d), d).start()

    for c in range(NCHUNK):
        def add_slot(d, total):
            z = z_peer(d)
            z_arrived(c, z).wait_recv()
            return total + z_recv[c, z].astype(F32)

        own_part = half_own[c, rows((z_lo * 2 + z_hi) * OWN, OWN)]
        grad_ref[:, c * CHUNK : (c + 1) * CHUNK] = lax.fori_loop(1, NZ, add_slot, own_part)

    kv_copy(my_rows, ctx, 0, kv_ss, zh_dev).wait_send()
    zkv.wait_send()

    @pl.loop(1, NXY)
    def _(d):
        k = plane_peer(d)
        kv_copy(my_rows, ctx, d, kv_ss, plane_dev(k)).wait_send()
        kv_copy(other_rows, ctx_other, d, kvz_ss, plane_dev(k)).wait_send()
        pltpu.make_async_copy(x_recv.at[k], x_recv.at[k], x_ss.at[d]).wait()
        dkv_copy(dkv_send, dkv_recv, dkv_ss, dkv_rs, plane, k, d, plane_dev).wait_send()
        for c in range(NCHUNK):
            g_copy(c, k, d).wait_send()

    for c in range(NCHUNK):
        core_copy(c).wait_send()

        @pl.loop(1, NZ)
        def _(d):
            z_copy(c, z_peer(d), d).wait_send()


def dkv_copy(send, recv, ss, rs, source, k, d, plane_dev):
    return pltpu.make_async_remote_copy(
        src_ref=send.at[pl.ds(pl.multiple_of(k * 2 * TOK, 2 * TOK), 2 * TOK)],
        dst_ref=recv.at[source],
        send_sem=ss.at[d],
        recv_sem=rs.at[source],
        device_id=plane_dev(k),
        device_id_type=MESH,
    )


def fused(order, x, q, k, v, o):
    vmem = pl.BlockSpec(memory_space=pltpu.VMEM)
    dma = pltpu.SemaphoreType.DMA
    scratch = [
        pltpu.VMEM((KEYS, 2 * HD), BF16),
        pltpu.VMEM((HD, KEYS), BF16),
        pltpu.VMEM((NXY, 8, TOK, TOK), BF16),
        pltpu.VMEM((ROWS, NXY * TOK), BF16),
        pltpu.VMEM((KEYS, CHUNK), F32),
        pltpu.VMEM((KEYS, CHUNK), F32),
        pltpu.VMEM((KEYS, 2 * HD), F32),
        pltpu.VMEM((KEYS, 2 * HD), BF16),
        pltpu.VMEM((NXY, 2 * TOK, 2 * HD), BF16),
        pltpu.VMEM((2 * TOK, 2 * HD), BF16),
        pltpu.VMEM((TOK, 2 * HD), BF16),
        pltpu.VMEM((NCHUNK, NXY * TOK, CHUNK), BF16),
        pltpu.VMEM((NCHUNK, ROWS // 2, CHUNK), F32),
        pltpu.VMEM((NCHUNK, ROWS // 2, CHUNK), F32),
        pltpu.VMEM((NCHUNK, ROWS // 2, CHUNK), F32),
        pltpu.VMEM((NCHUNK, NZ, OWN, CHUNK), BF16),
        pltpu.VMEM((NCHUNK, NZ, OWN, CHUNK), BF16),
        dma((NXY,)),
        dma((NCTX,)),
        dma((NXY,)),
        dma((NXY,)),
        dma((NXY,)),
        dma((NCHUNK, NXY)),
        dma((NCHUNK, NXY)),
        dma((NXY,)),
        dma((NXY,)),
        dma,
        dma,
        dma((NCHUNK,)),
        dma((NCHUNK,)),
        dma((NCHUNK, NZ)),
        dma((NCHUNK, NZ)),
    ]
    return pl.pallas_call(
        fused_kernel,
        name="attention_backward_and_weight_gradient",
        out_shape=jax.ShapeDtypeStruct((OWN, NCHUNK * CHUNK), F32),
        in_specs=[
            pl.BlockSpec(memory_space=pltpu.SMEM),
            pl.BlockSpec(memory_space=pl.ANY),
            vmem,
            vmem,
            vmem,
            vmem,
        ],
        out_specs=vmem,
        scratch_shapes=scratch,
        compiler_params=pltpu.CompilerParams(
            collective_id=0, has_side_effects=True, vmem_limit_bytes=60 * 2**20
        ),
    )(order, x, q, k, v, o)


def per_device(
    layer_input,
    query_rows,
    key_rows,
    value_rows,
    out_grad,
    block_order,
    master,
    moment_one,
    moment_two,
):
    grad_local = fused(
        block_order, layer_input[0], query_rows[0], key_rows[0], value_rows[0], out_grad[0]
    )
    new_one = BETA_ONE * moment_one + (1.0 - BETA_ONE) * grad_local
    new_two = BETA_TWO * moment_two + (1.0 - BETA_TWO) * grad_local * grad_local
    corr_one = 1.0 - BETA_ONE**STEP
    corr_two = 1.0 - BETA_TWO**STEP
    update = new_one / corr_one / (jnp.sqrt(new_two / corr_two) + EPSILON)
    new_master = master - LEARN_RATE * (update + DECAY * master)
    return (new_master, new_one, new_two)


def solution(mesh):
    rows = P("dp", "ctx", None)
    owned = P(("dp", "ctx"), None)
    return jax.shard_map(
        per_device,
        mesh=mesh,
        in_specs=(rows, rows, rows, rows, rows, P(), owned, owned, owned),
        out_specs=(owned, owned, owned),
        check_vma=False,
    )
```

```python
import functools
import math

import jax
import jax.numpy as jnp
from jax import lax
from jax.experimental import pallas as pl
from jax.experimental.pallas import tpu as pltpu
from jax.sharding import PartitionSpec as P

STEP = 10
NEG_FILL = -1e30
BETA_ONE = 0.9
BETA_TWO = 0.95
EPSILON = 1e-08
LEARN_RATE = 0.01
DECAY = 0.1

F32 = jnp.float32
BF16 = jnp.bfloat16
MESH = pl.DeviceIdType.MESH
ROW_CONTRACT = (((1,), (1,)), ((), ()))

TOK = 128
HD = 128
HALF = 64
NXY = 16
NCTX = 32
NZ = 8
CHUNK = 256
NCHUNK = 5
KEYS = NCTX * TOK
KT = 512
OWN = 64
ROWS = 1024
SCALE = 1.0 / math.sqrt(HD)


def fused_kernel(
    order_ref,
    x_hbm,
    q_ref,
    k_ref,
    v_ref,
    o_ref,
    grad_ref,
    kv_all,
    k_t,
    x_recv,
    x_t,
    s_scr,
    d_scr,
    dkv_acc,
    dkv_send,
    dkv_one,
    dkv_sum,
    dkv_two,
    zkv_send,
    zkv_recv,
    g_all,
    core_send,
    core_recv,
    half_own,
    z_send,
    z_recv,
    kvz_ss,
    kvz_rs,
    kv1_ss,
    kv1_rs,
    kv2_ss,
    kv2_rs,
    x_ss,
    x_rs,
    g1_ss,
    g1_rs,
    g2_ss,
    g2_rs,
    dkv1_ss,
    dkv1_rs,
    dkv2_ss,
    dkv2_rs,
    zkv_ss,
    zkv_rs,
    core_ss,
    core_rs,
    z_ss,
    z_rs,
):
    dp = lax.axis_index("dp")
    ctx = lax.axis_index("ctx")
    core = lax.rem(dp, 2)
    z_lo = dp // 2
    z_hi = lax.rem(ctx, 2)
    plane = ctx // 2
    y = plane // 4
    x = lax.rem(plane, 4)
    z_me = z_hi * 4 + z_lo

    def plane_peer(d):
        return lax.rem(y + d // 4, 4) * 4 + lax.rem(x + lax.rem(d, 4), 4)

    def plane_dev(k):
        return (dp, k * 2 + z_hi)

    def z_peer(d):
        return lax.rem(z_me + d, NZ)

    def z_dev(z):
        return (lax.rem(z, 4) * 2 + core, plane * 2 + z // 4)

    zh_dev = (dp, plane * 2 + (1 - z_hi))
    place = (y, x)

    def line_dev(axis, i):
        return plane_dev(i * 4 + x if axis == 0 else y * 4 + i)

    def line_peer(axis, d):
        return lax.rem(place[axis] + d, 4)

    def remote(src, dst, ss, rs, target):
        return pltpu.make_async_remote_copy(
            src_ref=src,
            dst_ref=dst,
            send_sem=ss,
            recv_sem=rs,
            device_id=target,
            device_id_type=MESH,
        )

    def across(array, half, i):
        return array.at[half, :, i] if half == 0 else array.at[half, i]

    core_dev = (z_lo * 2 + (1 - core), ctx)

    barrier = pltpu.get_barrier_semaphore()

    @pl.loop(1, NXY)
    def _(d):
        pl.semaphore_signal(barrier, inc=1, device_id=plane_dev(plane_peer(d)), device_id_type=MESH)

    @pl.loop(1, NZ)
    def _(d):
        pl.semaphore_signal(barrier, inc=1, device_id=z_dev(z_peer(d)), device_id_type=MESH)

    pl.semaphore_signal(barrier, inc=1, device_id=core_dev, device_id_type=MESH)

    def rows(first, count):
        return pl.ds(pl.multiple_of(first, count), count)

    kv_all[0, y, x, z_hi] = k_ref[...]
    kv_all[1, y, x, z_hi] = v_ref[...]

    pl.semaphore_wait(barrier, NXY - 1 + NZ - 1 + 1)

    kvz = remote(
        kv_all.at[:, y, x, z_hi], kv_all.at[:, y, x, z_hi], kvz_ss, kvz_rs, zh_dev
    )

    def kv_one(z, half, d):
        piece = kv_all.at[half, y, x, z]
        return remote(
            piece,
            piece,
            kv1_ss.at[z, half, d],
            kv1_rs.at[z, half, place[half]],
            line_dev(half, line_peer(half, d)),
        )

    def kv_one_arrived(z, half, d):
        i = line_peer(half, d)
        piece = kv_all.at[half, i, x, z] if half == 0 else kv_all.at[half, y, i, z]
        return remote(
            piece, piece, kv1_ss.at[z, half, d], kv1_rs.at[z, half, i], line_dev(half, i)
        )

    def kv_line(z, half, i):
        return kv_all.at[half, :, i, z] if half == 0 else kv_all.at[half, i, :, z]

    def kv_two(z, half, d):
        axis = 1 - half
        piece = kv_line(z, half, place[axis])
        return remote(
            piece,
            piece,
            kv2_ss.at[z, half, d],
            kv2_rs.at[z, half, place[axis]],
            line_dev(axis, line_peer(axis, d)),
        )

    def kv_two_arrived(z, half, d):
        axis = 1 - half
        i = line_peer(axis, d)
        piece = kv_line(z, half, i)
        return remote(
            piece, piece, kv2_ss.at[z, half, d], kv2_rs.at[z, half, i], line_dev(axis, i)
        )

    steps = [(half, d) for d in (1, 3, 2) for half in (0, 1)]
    kvz.start()
    for half, d in steps:
        kv_one(z_hi, half, d).start()
    kvz.wait_recv()
    for half, d in steps:
        kv_one(1 - z_hi, half, d).start()
    for z in (z_hi, 1 - z_hi):
        for half in (0, 1):
            for d in (1, 3, 2):
                kv_one_arrived(z, half, d).wait_recv()
            for d in (1, 3, 2):
                kv_two(z, half, d).start()
    for z in (z_hi, 1 - z_hi):
        for half, d in steps:
            kv_two_arrived(z, half, d).wait_recv()

    def x_copy(k, j, d):
        column = ((j % 4) * 2 + j // 4) * (NCTX * OWN) + k * TOK
        return pltpu.make_async_remote_copy(
            src_ref=x_hbm.at[:, rows(column, TOK)],
            dst_ref=x_recv.at[plane, j],
            send_sem=x_ss.at[d],
            recv_sem=x_rs.at[plane],
            device_id=plane_dev(k),
            device_id_type=MESH,
        )

    def x_own(j):
        column = ((j % 4) * 2 + j // 4) * (NCTX * OWN) + plane * TOK
        return pltpu.make_async_copy(
            x_hbm.at[:, rows(column, TOK)], x_recv.at[plane, j], x_rs.at[plane]
        )

    @pl.loop(1, NXY)
    def _(d):
        for j in range(8):
            x_copy(plane_peer(d), j, d).start()

    for j in range(8):
        x_own(j).start()

    lane = lax.broadcasted_iota(jnp.int32, (1, CHUNK), 1)
    token = lax.rem(lane, TOK)
    query_pos = (
        jnp.where(token < HALF, order_ref[2 * ctx], order_ref[2 * ctx + 1]) * HALF
        + lax.rem(token, HALF)
    )
    sub = lax.broadcasted_iota(jnp.int32, (HALF, CHUNK), 0)

    @pl.loop(0, NCTX)
    def _(b):
        k_t[:, rows(b * TOK, TOK)] = kv_all[0, b // 8, lax.rem(b // 2, 4), lax.rem(b, 2)].T

    def g_one(chunk, half, d):
        piece = g_all.at[chunk, half, y, x]
        return remote(
            piece,
            piece,
            g1_ss.at[chunk, half, d],
            g1_rs.at[chunk, half, place[half]],
            line_dev(half, line_peer(half, d)),
        )

    def g_one_arrived(chunk, half, d):
        i = line_peer(half, d)
        piece = g_all.at[chunk, half, i, x] if half == 0 else g_all.at[chunk, half, y, i]
        return remote(
            piece, piece, g1_ss.at[chunk, half, d], g1_rs.at[chunk, half, i], line_dev(half, i)
        )

    def g_two(chunk, half, d):
        axis = 1 - half
        piece = across(g_all.at[chunk], half, place[axis])
        return remote(
            piece,
            piece,
            g2_ss.at[chunk, half, d],
            g2_rs.at[chunk, half, place[axis]],
            line_dev(axis, line_peer(axis, d)),
        )

    def g_two_arrived(chunk, half, d):
        axis = 1 - half
        i = line_peer(axis, d)
        piece = across(g_all.at[chunk], half, i)
        return remote(
            piece, piece, g2_ss.at[chunk, half, d], g2_rs.at[chunk, half, i], line_dev(axis, i)
        )

    def send_chunk(chunk):
        for half, d in steps:
            g_one(chunk, half, d).start()

    def forward_chunk(chunk):
        for half in (0, 1):
            for d in (1, 3, 2):
                g_one_arrived(chunk, half, d).wait_recv()
            for d in (1, 3, 2):
                g_two(chunk, half, d).start()

    def dkv_first(half, d):
        i = line_peer(half, d)
        return remote(
            dkv_send.at[half, i] if half == 0 else dkv_send.at[half, :, i],
            dkv_one.at[half, place[half]],
            dkv1_ss.at[half, d],
            dkv1_rs.at[half, place[half]],
            line_dev(half, i),
        )

    def dkv_first_arrived(half, d):
        i = line_peer(half, d)
        return remote(
            dkv_one.at[half, i],
            dkv_one.at[half, i],
            dkv1_ss.at[half, d],
            dkv1_rs.at[half, i],
            line_dev(half, i),
        )

    def dkv_second(half, d):
        axis = 1 - half
        i = line_peer(axis, d)
        return remote(
            dkv_sum.at[half, i],
            dkv_two.at[half, place[axis]],
            dkv2_ss.at[half, d],
            dkv2_rs.at[half, place[axis]],
            line_dev(axis, i),
        )

    def dkv_second_arrived(half, d):
        axis = 1 - half
        i = line_peer(axis, d)
        return remote(
            dkv_two.at[half, i],
            dkv_two.at[half, i],
            dkv2_ss.at[half, d],
            dkv2_rs.at[half, i],
            line_dev(axis, i),
        )

    def key_tile(ref, half, t):
        return ref.at[half, t // 2, pl.ds(lax.rem(t, 2) * 2, 2)]

    def fold(a, op):
        return op(a.reshape(a.shape[0] // 8, 8, a.shape[1]), axis=0)

    for c in range(4):
        heads = (2 * c, 2 * c + 1)
        q_c = jnp.concatenate([q_ref[:, h * HD : (h + 1) * HD] for h in heads], axis=0)
        o_c = jnp.concatenate([o_ref[:, h * HD : (h + 1) * HD] for h in heads], axis=0)

        def scores_tile(t, top):
            first = pl.multiple_of(t * KT, KT)
            s = lax.dot_general(
                key_tile(kv_all, 0, t)[...].reshape(KT, HD), q_c, ROW_CONTRACT, preferred_element_type=F32
            )
            d_scr[pl.ds(first, KT)] = lax.dot_general(
                key_tile(kv_all, 1, t)[...].reshape(KT, HD), o_c, ROW_CONTRACT, preferred_element_type=F32
            )
            for b in range(KT // HALF):
                limit = query_pos - order_ref[t * (KT // HALF) + b] * HALF
                part = jnp.where(sub <= limit, s[b * HALF : (b + 1) * HALF], NEG_FILL)
                s_scr[pl.ds(first + b * HALF, HALF)] = part
                top = jnp.maximum(top, fold(part, jnp.max))
            return top

        top = lax.fori_loop(0, KEYS // KT, scores_tile, jnp.full((8, CHUNK), NEG_FILL, F32))
        top = jnp.max(top, axis=0, keepdims=True)

        def weights_tile(t, carried):
            total, inner = carried
            tile = pl.ds(pl.multiple_of(t * KT, KT), KT)
            e = jnp.exp2((s_scr[tile] - top) * (SCALE * math.log2(math.e)))
            s_scr[tile] = e
            return total + fold(e, jnp.sum), inner + fold(e * d_scr[tile], jnp.sum)

        zero = jnp.zeros((8, CHUNK), F32)
        total, inner = lax.fori_loop(0, KEYS // KT, weights_tile, (zero, zero))
        inv = 1.0 / jnp.sum(total, axis=0, keepdims=True)
        delta = jnp.sum(inner, axis=0, keepdims=True) * inv

        def grads_tile(t, dq):
            first = pl.multiple_of(t * KT, KT)
            tile = pl.ds(first, KT)
            p = s_scr[tile] * inv
            ds = (p * (d_scr[tile] - delta) * SCALE).astype(BF16)
            dk = jnp.dot(ds, q_c, preferred_element_type=F32)
            dv = jnp.dot(p.astype(BF16), o_c, preferred_element_type=F32)
            if c == 0:
                dkv_acc[tile, :HD] = dk
                dkv_acc[tile, HD:] = dv
            elif c < 3:
                dkv_acc[tile, :HD] += dk
                dkv_acc[tile, HD:] += dv
            else:
                dk = (dkv_acc[tile, :HD] + dk).astype(BF16)
                dv = (dkv_acc[tile, HD:] + dv).astype(BF16)
                key_tile(dkv_send, 0, t)[...] = dk.reshape(2, 2, TOK, HD)
                key_tile(dkv_send, 1, t)[...] = dv.reshape(2, 2, TOK, HD)
            return dq + jnp.dot(k_t[:, tile], ds, preferred_element_type=F32)

        dq = lax.fori_loop(0, KEYS // KT, grads_tile, jnp.zeros((HD, CHUNK), F32))
        for i in range(2):
            g_all[c, i, y, x] = dq[:, i * TOK : (i + 1) * TOK].T.astype(BF16)
        if c == 3:
            for half, d in steps:
                dkv_first(half, d).start()
        send_chunk(c)
        if c > 0:
            forward_chunk(c - 1)

    for half in (0, 1):
        for d in (1, 3, 2):
            dkv_first_arrived(half, d).wait_recv()
        for j in range(4):
            piece = dkv_send[half, y, j] if half == 0 else dkv_send[half, j, x]
            total = piece.astype(F32)
            for d in (1, 3, 2):
                total += dkv_one[half, line_peer(half, d), j].astype(F32)
            dkv_sum[half, j] = total
        for d in (1, 3, 2):
            dkv_second(half, d).start()

    forward_chunk(3)

    for half in (0, 1):
        axis = 1 - half
        total = dkv_sum[half, place[axis]]
        for d in (1, 3, 2):
            dkv_second_arrived(half, d).wait_recv()
            total += dkv_two[half, line_peer(axis, d)]
        zkv_send[0, half] = total[0]
        zkv_send[1, half] = total[1]
    zkv = remote(zkv_send.at[1 - z_hi], zkv_recv, zkv_ss, zkv_rs, zh_dev)
    zkv.start()
    zkv.wait_recv()
    for half in (0, 1):
        g_all[4, half, y, x] = (zkv_send[z_hi, half] + zkv_recv[half]).astype(BF16)
    send_chunk(4)
    forward_chunk(4)

    for j in range(8):
        x_own(j).wait()

    def transpose_slot(k):
        for j in range(8):
            x_t[j * TOK : (j + 1) * TOK, rows(k * TOK, TOK)] = x_recv[k, j].T

    transpose_slot(plane)

    @pl.loop(1, NXY)
    def _(d):
        k = plane_peer(d)
        pltpu.make_async_copy(x_recv.at[k], x_recv.at[k], x_rs.at[k]).wait()
        transpose_slot(k)

    def z_copy(chunk, z, d):
        return pltpu.make_async_remote_copy(
            src_ref=z_send.at[chunk, z],
            dst_ref=z_recv.at[chunk, z_me],
            send_sem=z_ss.at[chunk, d],
            recv_sem=z_rs.at[chunk, z_me],
            device_id=z_dev(z),
            device_id_type=MESH,
        )

    def z_arrived(chunk, z):
        return pltpu.make_async_remote_copy(
            src_ref=z_send.at[chunk, z],
            dst_ref=z_recv.at[chunk, z],
            send_sem=z_ss.at[chunk, 0],
            recv_sem=z_rs.at[chunk, z],
            device_id=z_dev(z),
            device_id_type=MESH,
        )

    def core_copy(chunk):
        return pltpu.make_async_remote_copy(
            src_ref=core_send.at[chunk],
            dst_ref=core_recv.at[chunk],
            send_sem=core_ss.at[chunk],
            recv_sem=core_rs.at[chunk],
            device_id=core_dev,
            device_id_type=MESH,
        )

    for c in range(NCHUNK):
        for half, d in steps:
            g_two_arrived(c, half, d).wait_recv()
        columns = jnp.concatenate(
            [g_all[c, half].reshape(NXY * TOK, HD) for half in (0, 1)], axis=1
        )

        def product(first):
            return jnp.dot(
                x_t[pl.ds(pl.multiple_of(first, 256), 256)], columns, preferred_element_type=F32
            )

        @pl.loop(0, 2)
        def _(i):
            core_send[c, rows(i * 256, 256)] = product((1 - core) * 512 + i * 256)

        core_copy(c).start()

        @pl.loop(0, 2)
        def _(i):
            half_own[c, rows(i * 256, 256)] = product(core * 512 + i * 256)

        core_copy(c).wait_recv()
        for j in range(NZ):
            z = (j % 2) * 4 + j // 2
            part = pl.ds(j * OWN, OWN)
            total = half_own[c, part] + core_recv[c, part]
            half_own[c, part] = total
            z_send[c, z] = total.astype(BF16)

        @pl.loop(1, NZ)
        def _(d):
            z_copy(c, z_peer(d), d).start()

    for c in range(NCHUNK):
        def add_slot(d, total):
            z = z_peer(d)
            z_arrived(c, z).wait_recv()
            return total + z_recv[c, z].astype(F32)

        own_part = half_own[c, rows((z_lo * 2 + z_hi) * OWN, OWN)]
        grad_ref[:, c * CHUNK : (c + 1) * CHUNK] = lax.fori_loop(1, NZ, add_slot, own_part)

    kvz.wait_send()
    zkv.wait_send()
    for half, d in steps:
        for z in (z_hi, 1 - z_hi):
            kv_one(z, half, d).wait_send()
            kv_two(z, half, d).wait_send()
        dkv_first(half, d).wait_send()
        dkv_second(half, d).wait_send()
        for c in range(NCHUNK):
            g_one(c, half, d).wait_send()
            g_two(c, half, d).wait_send()

    @pl.loop(1, NXY)
    def _(d):
        k = plane_peer(d)
        pltpu.make_async_copy(x_recv.at[k], x_recv.at[k], x_ss.at[d]).wait()

    for c in range(NCHUNK):
        core_copy(c).wait_send()

        @pl.loop(1, NZ)
        def _(d):
            z_copy(c, z_peer(d), d).wait_send()


def fused(order, x, q, k, v, o):
    vmem = pl.BlockSpec(memory_space=pltpu.VMEM)
    dma = pltpu.SemaphoreType.DMA
    scratch = [
        pltpu.VMEM((2, 4, 4, 2, TOK, HD), BF16),
        pltpu.VMEM((HD, KEYS), BF16),
        pltpu.VMEM((NXY, 8, TOK, TOK), BF16),
        pltpu.VMEM((ROWS, NXY * TOK), BF16),
        pltpu.VMEM((KEYS, CHUNK), F32),
        pltpu.VMEM((KEYS, CHUNK), F32),
        pltpu.VMEM((KEYS, 2 * HD), F32),
        pltpu.VMEM((2, 4, 4, 2, TOK, HD), BF16),
        pltpu.VMEM((2, 4, 4, 2, TOK, HD), BF16),
        pltpu.VMEM((2, 4, 2, TOK, HD), F32),
        pltpu.VMEM((2, 4, 2, TOK, HD), F32),
        pltpu.VMEM((2, 2, TOK, HD), F32),
        pltpu.VMEM((2, TOK, HD), F32),
        pltpu.VMEM((NCHUNK, 2, 4, 4, TOK, HD), BF16),
        pltpu.VMEM((NCHUNK, ROWS // 2, CHUNK), F32),
        pltpu.VMEM((NCHUNK, ROWS // 2, CHUNK), F32),
        pltpu.VMEM((NCHUNK, ROWS // 2, CHUNK), F32),
        pltpu.VMEM((NCHUNK, NZ, OWN, CHUNK), BF16),
        pltpu.VMEM((NCHUNK, NZ, OWN, CHUNK), BF16),
        dma,
        dma,
        dma((2, 2, 4)),
        dma((2, 2, 4)),
        dma((2, 2, 4)),
        dma((2, 2, 4)),
        dma((NXY,)),
        dma((NXY,)),
        dma((NCHUNK, 2, 4)),
        dma((NCHUNK, 2, 4)),
        dma((NCHUNK, 2, 4)),
        dma((NCHUNK, 2, 4)),
        dma((2, 4)),
        dma((2, 4)),
        dma((2, 4)),
        dma((2, 4)),
        dma,
        dma,
        dma((NCHUNK,)),
        dma((NCHUNK,)),
        dma((NCHUNK, NZ)),
        dma((NCHUNK, NZ)),
    ]
    return pl.pallas_call(
        fused_kernel,
        name="attention_backward_and_weight_gradient",
        out_shape=jax.ShapeDtypeStruct((OWN, NCHUNK * CHUNK), F32),
        in_specs=[
            pl.BlockSpec(memory_space=pltpu.SMEM),
            pl.BlockSpec(memory_space=pl.ANY),
            vmem,
            vmem,
            vmem,
            vmem,
        ],
        out_specs=vmem,
        scratch_shapes=scratch,
        compiler_params=pltpu.CompilerParams(
            collective_id=0, has_side_effects=True, vmem_limit_bytes=60 * 2**20
        ),
    )(order, x, q, k, v, o)


def per_device(
    layer_input,
    query_rows,
    key_rows,
    value_rows,
    out_grad,
    block_order,
    master,
    moment_one,
    moment_two,
):
    grad_local = fused(
        block_order, layer_input[0], query_rows[0], key_rows[0], value_rows[0], out_grad[0]
    )
    new_one = BETA_ONE * moment_one + (1.0 - BETA_ONE) * grad_local
    new_two = BETA_TWO * moment_two + (1.0 - BETA_TWO) * grad_local * grad_local
    corr_one = 1.0 - BETA_ONE**STEP
    corr_two = 1.0 - BETA_TWO**STEP
    update = new_one / corr_one / (jnp.sqrt(new_two / corr_two) + EPSILON)
    new_master = master - LEARN_RATE * (update + DECAY * master)
    return (new_master, new_one, new_two)


def solution(mesh):
    rows = P("dp", "ctx", None)
    owned = P(("dp", "ctx"), None)
    return jax.shard_map(
        per_device,
        mesh=mesh,
        in_specs=(rows, rows, rows, rows, rows, P(), owned, owned, owned),
        out_specs=(owned, owned, owned),
        check_vma=False,
    )
```

```python
import functools
import math

import jax
import jax.numpy as jnp
from jax import lax
from jax.experimental import pallas as pl
from jax.experimental.pallas import tpu as pltpu
from jax.sharding import PartitionSpec as P

STEP = 10
NEG_FILL = -1e30
BETA_ONE = 0.9
BETA_TWO = 0.95
EPSILON = 1e-08
LEARN_RATE = 0.01
DECAY = 0.1

F32 = jnp.float32
BF16 = jnp.bfloat16
MESH = pl.DeviceIdType.MESH
ROW_CONTRACT = (((1,), (1,)), ((), ()))

TOK = 128
HD = 128
HALF = 64
NXY = 16
NCTX = 32
NZ = 8
CHUNK = 256
NCHUNK = 5
KEYS = NCTX * TOK
KT = 512
OWN = 64
ROWS = 1024
SCALE = 1.0 / math.sqrt(HD)


def fused_kernel(
    order_ref,
    x_hbm,
    q_ref,
    k_ref,
    v_ref,
    o_ref,
    grad_ref,
    kv_all,
    k_t,
    x_mid,
    x_recv,
    x_t,
    s_scr,
    d_scr,
    dkv_acc,
    dkv_send,
    dkv_one,
    dkv_sum,
    dkv_two,
    zkv_send,
    zkv_recv,
    g_all,
    core_send,
    core_recv,
    half_own,
    z_send,
    z_recv,
    kvz_ss,
    kvz_rs,
    kv1_ss,
    kv1_rs,
    kv2_ss,
    kv2_rs,
    x0_ss,
    x1_ss,
    x1_rs,
    x2_ss,
    x_rs,
    x_own_sem,
    g1_ss,
    g1_rs,
    g2_ss,
    g2_rs,
    dkv1_ss,
    dkv1_rs,
    dkv2_ss,
    dkv2_rs,
    zkv_ss,
    zkv_rs,
    core_ss,
    core_rs,
    z_ss,
    z_rs,
):
    dp = lax.axis_index("dp")
    ctx = lax.axis_index("ctx")
    core = lax.rem(dp, 2)
    z_lo = dp // 2
    z_hi = lax.rem(ctx, 2)
    plane = ctx // 2
    y = plane // 4
    x = lax.rem(plane, 4)
    z_me = z_hi * 4 + z_lo

    def plane_peer(d):
        return lax.rem(y + d // 4, 4) * 4 + lax.rem(x + lax.rem(d, 4), 4)

    def plane_dev(k):
        return (dp, k * 2 + z_hi)

    def z_peer(d):
        return lax.rem(z_me + d, NZ)

    def z_dev(z):
        return (lax.rem(z, 4) * 2 + core, plane * 2 + z // 4)

    zh_dev = (dp, plane * 2 + (1 - z_hi))
    place = (y, x)

    def line_dev(axis, i):
        return plane_dev(i * 4 + x if axis == 0 else y * 4 + i)

    def line_peer(axis, d):
        return lax.rem(place[axis] + d, 4)

    def remote(src, dst, ss, rs, target):
        return pltpu.make_async_remote_copy(
            src_ref=src,
            dst_ref=dst,
            send_sem=ss,
            recv_sem=rs,
            device_id=target,
            device_id_type=MESH,
        )

    def across(array, half, i):
        return array.at[half, :, i] if half == 0 else array.at[half, i]

    core_dev = (z_lo * 2 + (1 - core), ctx)

    barrier = pltpu.get_barrier_semaphore()

    @pl.loop(1, NXY)
    def _(d):
        pl.semaphore_signal(barrier, inc=1, device_id=plane_dev(plane_peer(d)), device_id_type=MESH)

    @pl.loop(1, NZ)
    def _(d):
        pl.semaphore_signal(barrier, inc=1, device_id=z_dev(z_peer(d)), device_id_type=MESH)

    pl.semaphore_signal(barrier, inc=1, device_id=core_dev, device_id_type=MESH)

    def rows(first, count):
        return pl.ds(pl.multiple_of(first, count), count)

    kv_all[0, y, x, z_hi] = k_ref[...]
    kv_all[1, y, x, z_hi] = v_ref[...]

    pl.semaphore_wait(barrier, NXY - 1 + NZ - 1 + 1)

    kvz = remote(
        kv_all.at[:, y, x, z_hi], kv_all.at[:, y, x, z_hi], kvz_ss, kvz_rs, zh_dev
    )

    def kv_one(z, half, d):
        piece = kv_all.at[half, y, x, z]
        return remote(
            piece,
            piece,
            kv1_ss.at[z, half, d],
            kv1_rs.at[z, half, place[half]],
            line_dev(half, line_peer(half, d)),
        )

    def kv_one_arrived(z, half, d):
        i = line_peer(half, d)
        piece = kv_all.at[half, i, x, z] if half == 0 else kv_all.at[half, y, i, z]
        return remote(
            piece, piece, kv1_ss.at[z, half, d], kv1_rs.at[z, half, i], line_dev(half, i)
        )

    def kv_line(z, half, i):
        return kv_all.at[half, :, i, z] if half == 0 else kv_all.at[half, i, :, z]

    def kv_two(z, half, d):
        axis = 1 - half
        piece = kv_line(z, half, place[axis])
        return remote(
            piece,
            piece,
            kv2_ss.at[z, half, d],
            kv2_rs.at[z, half, place[axis]],
            line_dev(axis, line_peer(axis, d)),
        )

    def kv_two_arrived(z, half, d):
        axis = 1 - half
        i = line_peer(axis, d)
        piece = kv_line(z, half, i)
        return remote(
            piece, piece, kv2_ss.at[z, half, d], kv2_rs.at[z, half, i], line_dev(axis, i)
        )

    def x_columns(half, low, row, col):
        first = (low * 2 + half) * (NCTX * OWN) + (row * 4 + col) * TOK
        return x_hbm.at[:, rows(first, TOK)]

    def x_start(half, d):
        i = line_peer(half, d)
        for e in range(4):
            j = lax.rem(place[1 - half] + e, 4)
            for low in range(4):
                target = x_recv.at[half, y, x, low] if e == 0 else x_mid.at[half, place[half], j, low]
                remote(
                    x_columns(half, low, i, j) if half == 0 else x_columns(half, low, j, i),
                    target,
                    x1_ss.at[half, d],
                    x_rs.at[half, y, x] if e == 0 else x1_rs.at[half, place[half], j],
                    line_dev(half, i),
                ).start()

    def x_start_line(half, d):
        axis = 1 - half
        i = line_peer(axis, d)
        for low in range(4):
            remote(
                x_columns(half, low, y, i) if half == 0 else x_columns(half, low, i, x),
                x_recv.at[half, y, x, low],
                x0_ss.at[half, d],
                x_rs.at[half, y, x],
                line_dev(axis, i),
            ).start()

    def x_own(half, low):
        return pltpu.make_async_copy(
            x_columns(half, low, y, x), x_recv.at[half, y, x, low], x_own_sem.at[half, low]
        )

    def x_two(half, d, e):
        axis = 1 - half
        i = line_peer(half, d)
        j = line_peer(axis, e)
        where = (i, x) if half == 0 else (y, i)
        return remote(
            x_mid.at[half, i, j],
            x_recv.at[half, where[0], where[1]],
            x2_ss.at[half, d, e],
            x_rs.at[half, where[0], where[1]],
            line_dev(axis, j),
        )

    def x_forward(half):
        for d in (1, 3, 2):
            i = line_peer(half, d)
            for e in (1, 3, 2):
                j = line_peer(1 - half, e)
                piece = x_mid.at[half, i, j]
                pltpu.make_async_copy(piece, piece, x1_rs.at[half, i, j]).wait()
                x_two(half, d, e).start()

    steps = [(half, d) for d in (1, 3, 2) for half in (0, 1)]
    kvz.start()
    for half, d in steps:
        kv_one(z_hi, half, d).start()
    kvz.wait_recv()
    for half, d in steps:
        kv_one(1 - z_hi, half, d).start()
    for z in (z_hi, 1 - z_hi):
        for half in (0, 1):
            for d in (1, 3, 2):
                kv_one_arrived(z, half, d).wait_recv()
            for d in (1, 3, 2):
                kv_two(z, half, d).start()
    x_start(0, 1)
    x_start(1, 1)
    x_start(0, 3)
    x_start(1, 3)
    x_start(0, 2)
    x_start(1, 2)
    x_start_line(0, 1)
    x_start_line(1, 1)
    x_start_line(0, 3)
    x_start_line(1, 3)
    x_start_line(0, 2)
    x_start_line(1, 2)
    for half in (0, 1):
        for low in range(4):
            x_own(half, low).start()
    for z in (z_hi, 1 - z_hi):
        for half, d in steps:
            kv_two_arrived(z, half, d).wait_recv()

    lane = lax.broadcasted_iota(jnp.int32, (1, CHUNK), 1)
    token = lax.rem(lane, TOK)
    query_pos = (
        jnp.where(token < HALF, order_ref[2 * ctx], order_ref[2 * ctx + 1]) * HALF
        + lax.rem(token, HALF)
    )
    sub = lax.broadcasted_iota(jnp.int32, (HALF, CHUNK), 0)

    @pl.loop(0, NCTX)
    def _(b):
        k_t[:, rows(b * TOK, TOK)] = kv_all[0, b // 8, lax.rem(b // 2, 4), lax.rem(b, 2)].T

    def g_one(chunk, half, d):
        piece = g_all.at[chunk, half, y, x]
        return remote(
            piece,
            piece,
            g1_ss.at[chunk, half, d],
            g1_rs.at[chunk, half, place[half]],
            line_dev(half, line_peer(half, d)),
        )

    def g_one_arrived(chunk, half, d):
        i = line_peer(half, d)
        piece = g_all.at[chunk, half, i, x] if half == 0 else g_all.at[chunk, half, y, i]
        return remote(
            piece, piece, g1_ss.at[chunk, half, d], g1_rs.at[chunk, half, i], line_dev(half, i)
        )

    def g_two(chunk, half, d):
        axis = 1 - half
        piece = across(g_all.at[chunk], half, place[axis])
        return remote(
            piece,
            piece,
            g2_ss.at[chunk, half, d],
            g2_rs.at[chunk, half, place[axis]],
            line_dev(axis, line_peer(axis, d)),
        )

    def g_two_arrived(chunk, half, d):
        axis = 1 - half
        i = line_peer(axis, d)
        piece = across(g_all.at[chunk], half, i)
        return remote(
            piece, piece, g2_ss.at[chunk, half, d], g2_rs.at[chunk, half, i], line_dev(axis, i)
        )

    def send_chunk(chunk):
        for half, d in steps:
            g_one(chunk, half, d).start()

    def forward_chunk(chunk):
        for half in (0, 1):
            for d in (1, 3, 2):
                g_one_arrived(chunk, half, d).wait_recv()
            for d in (1, 3, 2):
                g_two(chunk, half, d).start()

    def dkv_first(half, d):
        i = line_peer(half, d)
        return remote(
            dkv_send.at[half, i] if half == 0 else dkv_send.at[half, :, i],
            dkv_one.at[half, place[half]],
            dkv1_ss.at[half, d],
            dkv1_rs.at[half, place[half]],
            line_dev(half, i),
        )

    def dkv_first_arrived(half, d):
        i = line_peer(half, d)
        return remote(
            dkv_one.at[half, i],
            dkv_one.at[half, i],
            dkv1_ss.at[half, d],
            dkv1_rs.at[half, i],
            line_dev(half, i),
        )

    def dkv_second(half, d):
        axis = 1 - half
        i = line_peer(axis, d)
        return remote(
            dkv_sum.at[half, i],
            dkv_two.at[half, place[axis]],
            dkv2_ss.at[half, d],
            dkv2_rs.at[half, place[axis]],
            line_dev(axis, i),
        )

    def dkv_second_arrived(half, d):
        axis = 1 - half
        i = line_peer(axis, d)
        return remote(
            dkv_two.at[half, i],
            dkv_two.at[half, i],
            dkv2_ss.at[half, d],
            dkv2_rs.at[half, i],
            line_dev(axis, i),
        )

    def key_tile(ref, half, t):
        return ref.at[half, t // 2, pl.ds(lax.rem(t, 2) * 2, 2)]

    def fold(a, op):
        return op(a.reshape(a.shape[0] // 8, 8, a.shape[1]), axis=0)

    for c in range(4):
        heads = (2 * c, 2 * c + 1)
        q_c = jnp.concatenate([q_ref[:, h * HD : (h + 1) * HD] for h in heads], axis=0)
        o_c = jnp.concatenate([o_ref[:, h * HD : (h + 1) * HD] for h in heads], axis=0)

        def scores_tile(t, top):
            first = pl.multiple_of(t * KT, KT)
            s = lax.dot_general(
                key_tile(kv_all, 0, t)[...].reshape(KT, HD), q_c, ROW_CONTRACT, preferred_element_type=F32
            )
            d_scr[pl.ds(first, KT)] = lax.dot_general(
                key_tile(kv_all, 1, t)[...].reshape(KT, HD), o_c, ROW_CONTRACT, preferred_element_type=F32
            )
            for b in range(KT // HALF):
                limit = query_pos - order_ref[t * (KT // HALF) + b] * HALF
                part = jnp.where(sub <= limit, s[b * HALF : (b + 1) * HALF], NEG_FILL)
                s_scr[pl.ds(first + b * HALF, HALF)] = part
                top = jnp.maximum(top, fold(part, jnp.max))
            return top

        top = lax.fori_loop(0, KEYS // KT, scores_tile, jnp.full((8, CHUNK), NEG_FILL, F32))
        top = jnp.max(top, axis=0, keepdims=True)

        def weights_tile(t, carried):
            total, inner = carried
            tile = pl.ds(pl.multiple_of(t * KT, KT), KT)
            e = jnp.exp2((s_scr[tile] - top) * (SCALE * math.log2(math.e)))
            s_scr[tile] = e
            return total + fold(e, jnp.sum), inner + fold(e * d_scr[tile], jnp.sum)

        zero = jnp.zeros((8, CHUNK), F32)
        total, inner = lax.fori_loop(0, KEYS // KT, weights_tile, (zero, zero))
        inv = 1.0 / jnp.sum(total, axis=0, keepdims=True)
        delta = jnp.sum(inner, axis=0, keepdims=True) * inv

        def grads_tile(t, dq):
            first = pl.multiple_of(t * KT, KT)
            tile = pl.ds(first, KT)
            p = s_scr[tile] * inv
            ds = (p * (d_scr[tile] - delta) * SCALE).astype(BF16)
            dk = jnp.dot(ds, q_c, preferred_element_type=F32)
            dv = jnp.dot(p.astype(BF16), o_c, preferred_element_type=F32)
            if c == 0:
                dkv_acc[tile, :HD] = dk
                dkv_acc[tile, HD:] = dv
            elif c < 3:
                dkv_acc[tile, :HD] += dk
                dkv_acc[tile, HD:] += dv
            else:
                dk = (dkv_acc[tile, :HD] + dk).astype(BF16)
                dv = (dkv_acc[tile, HD:] + dv).astype(BF16)
                key_tile(dkv_send, 0, t)[...] = dk.reshape(2, 2, TOK, HD)
                key_tile(dkv_send, 1, t)[...] = dv.reshape(2, 2, TOK, HD)
            return dq + jnp.dot(k_t[:, tile], ds, preferred_element_type=F32)

        dq = lax.fori_loop(0, KEYS // KT, grads_tile, jnp.zeros((HD, CHUNK), F32))
        for i in range(2):
            g_all[c, i, y, x] = dq[:, i * TOK : (i + 1) * TOK].T.astype(BF16)
        if c == 3:
            for half, d in steps:
                dkv_first(half, d).start()
        send_chunk(c)
        if c == 1:
            x_forward(0)
            x_forward(1)
        if c > 0:
            forward_chunk(c - 1)

    forward_chunk(3)

    for half in (0, 1):
        for d in (1, 3, 2):
            dkv_first_arrived(half, d).wait_recv()
        for j in range(4):
            piece = dkv_send[half, y, j] if half == 0 else dkv_send[half, j, x]
            total = piece.astype(F32)
            for d in (1, 3, 2):
                total += dkv_one[half, line_peer(half, d), j].astype(F32)
            dkv_sum[half, j] = total
        for d in (1, 3, 2):
            dkv_second(half, d).start()

    for half in (0, 1):
        axis = 1 - half
        total = dkv_sum[half, place[axis]]
        for d in (1, 3, 2):
            dkv_second_arrived(half, d).wait_recv()
            total += dkv_two[half, line_peer(axis, d)]
        zkv_send[0, half] = total[0]
        zkv_send[1, half] = total[1]
    zkv = remote(zkv_send.at[1 - z_hi], zkv_recv, zkv_ss, zkv_rs, zh_dev)
    zkv.start()

    def transpose_slot(row, col):
        for half in (0, 1):
            for low in range(4):
                first = (half * 4 + low) * TOK
                x_t[first : first + TOK, rows((row * 4 + col) * TOK, TOK)] = x_recv[
                    half, row, col, low
                ].T

    for half in (0, 1):
        for low in range(4):
            x_own(half, low).wait()
    transpose_slot(y, x)

    @pl.loop(1, NXY)
    def _(d):
        k = plane_peer(d)
        row, col = k // 4, lax.rem(k, 4)
        for half in (0, 1):
            piece = x_recv.at[half, row, col]
            pltpu.make_async_copy(piece, piece, x_rs.at[half, row, col]).wait()
        transpose_slot(row, col)

    def z_copy(chunk, z, d):
        return remote(
            z_send.at[chunk, z],
            z_recv.at[chunk, z_me],
            z_ss.at[chunk, d],
            z_rs.at[chunk, z_me],
            z_dev(z),
        )

    def z_arrived(chunk, z):
        return remote(
            z_send.at[chunk, z],
            z_recv.at[chunk, z],
            z_ss.at[chunk, 0],
            z_rs.at[chunk, z],
            z_dev(z),
        )

    def core_copy(chunk):
        return remote(
            core_send.at[chunk],
            core_recv.at[chunk],
            core_ss.at[chunk],
            core_rs.at[chunk],
            core_dev,
        )

    def multiply(c):
        for half, d in steps:
            g_two_arrived(c, half, d).wait_recv()
        columns = jnp.concatenate(
            [g_all[c, half].reshape(NXY * TOK, HD) for half in (0, 1)], axis=1
        )

        def product(first):
            return jnp.dot(
                x_t[pl.ds(pl.multiple_of(first, 256), 256)], columns, preferred_element_type=F32
            )

        @pl.loop(0, 2)
        def _(i):
            core_send[c, rows(i * 256, 256)] = product((1 - core) * 512 + i * 256)

        core_copy(c).start()

        @pl.loop(0, 2)
        def _(i):
            half_own[c, rows(i * 256, 256)] = product(core * 512 + i * 256)

    def reduce_cores(c):
        core_copy(c).wait_recv()
        for j in range(NZ):
            z = (j % 2) * 4 + j // 2
            part = pl.ds(j * OWN, OWN)
            total = half_own[c, part] + core_recv[c, part]
            half_own[c, part] = total
            z_send[c, z] = total.astype(BF16)

        @pl.loop(1, NZ)
        def _(d):
            z_copy(c, z_peer(d), d).start()

    multiply(0)
    multiply(1)
    reduce_cores(0)
    zkv.wait_recv()
    for half in (0, 1):
        g_all[4, half, y, x] = (zkv_send[z_hi, half] + zkv_recv[half]).astype(BF16)
    send_chunk(4)
    reduce_cores(1)
    multiply(2)
    forward_chunk(4)
    multiply(3)
    reduce_cores(2)
    reduce_cores(3)
    multiply(4)
    reduce_cores(4)

    for c in range(NCHUNK):
        def add_slot(d, total):
            z = z_peer(d)
            z_arrived(c, z).wait_recv()
            return total + z_recv[c, z].astype(F32)

        own_part = half_own[c, rows((z_lo * 2 + z_hi) * OWN, OWN)]
        grad_ref[:, c * CHUNK : (c + 1) * CHUNK] = lax.fori_loop(1, NZ, add_slot, own_part)

    kvz.wait_send()
    zkv.wait_send()
    for half, d in steps:
        for z in (z_hi, 1 - z_hi):
            kv_one(z, half, d).wait_send()
            kv_two(z, half, d).wait_send()
        dkv_first(half, d).wait_send()
        dkv_second(half, d).wait_send()
        for c in range(NCHUNK):
            g_one(c, half, d).wait_send()
            g_two(c, half, d).wait_send()
        pltpu.make_async_copy(x_mid.at[0, 0], x_mid.at[0, 0], x1_ss.at[half, d]).wait()
        pltpu.make_async_copy(x_recv.at[0, 0, 0], x_recv.at[0, 0, 0], x0_ss.at[half, d]).wait()
        for e in (1, 2, 3):
            x_two(half, d, e).wait_send()

    for c in range(NCHUNK):
        core_copy(c).wait_send()

        @pl.loop(1, NZ)
        def _(d):
            z_copy(c, z_peer(d), d).wait_send()


def fused(order, x, q, k, v, o):
    vmem = pl.BlockSpec(memory_space=pltpu.VMEM)
    dma = pltpu.SemaphoreType.DMA
    scratch = [
        pltpu.VMEM((2, 4, 4, 2, TOK, HD), BF16),
        pltpu.VMEM((HD, KEYS), BF16),
        pltpu.VMEM((2, 4, 4, 4, TOK, TOK), BF16),
        pltpu.VMEM((2, 4, 4, 4, TOK, TOK), BF16),
        pltpu.VMEM((ROWS, NXY * TOK), BF16),
        pltpu.VMEM((KEYS, CHUNK), F32),
        pltpu.VMEM((KEYS, CHUNK), F32),
        pltpu.VMEM((KEYS, 2 * HD), F32),
        pltpu.VMEM((2, 4, 4, 2, TOK, HD), BF16),
        pltpu.VMEM((2, 4, 4, 2, TOK, HD), BF16),
        pltpu.VMEM((2, 4, 2, TOK, HD), F32),
        pltpu.VMEM((2, 4, 2, TOK, HD), F32),
        pltpu.VMEM((2, 2, TOK, HD), F32),
        pltpu.VMEM((2, TOK, HD), F32),
        pltpu.VMEM((NCHUNK, 2, 4, 4, TOK, HD), BF16),
        pltpu.VMEM((NCHUNK, ROWS // 2, CHUNK), F32),
        pltpu.VMEM((NCHUNK, ROWS // 2, CHUNK), F32),
        pltpu.VMEM((NCHUNK, ROWS // 2, CHUNK), F32),
        pltpu.VMEM((NCHUNK, NZ, OWN, CHUNK), BF16),
        pltpu.VMEM((NCHUNK, NZ, OWN, CHUNK), BF16),
        dma,
        dma,
        dma((2, 2, 4)),
        dma((2, 2, 4)),
        dma((2, 2, 4)),
        dma((2, 2, 4)),
        dma((2, 4)),
        dma((2, 4)),
        dma((2, 4, 4)),
        dma((2, 4, 4)),
        dma((2, 4, 4)),
        dma((2, 4)),
        dma((NCHUNK, 2, 4)),
        dma((NCHUNK, 2, 4)),
        dma((NCHUNK, 2, 4)),
        dma((NCHUNK, 2, 4)),
        dma((2, 4)),
        dma((2, 4)),
        dma((2, 4)),
        dma((2, 4)),
        dma,
        dma,
        dma((NCHUNK,)),
        dma((NCHUNK,)),
        dma((NCHUNK, NZ)),
        dma((NCHUNK, NZ)),
    ]
    return pl.pallas_call(
        fused_kernel,
        name="attention_backward_and_weight_gradient",
        out_shape=jax.ShapeDtypeStruct((OWN, NCHUNK * CHUNK), F32),
        in_specs=[
            pl.BlockSpec(memory_space=pltpu.SMEM),
            pl.BlockSpec(memory_space=pl.ANY),
            vmem,
            vmem,
            vmem,
            vmem,
        ],
        out_specs=vmem,
        scratch_shapes=scratch,
        compiler_params=pltpu.CompilerParams(
            collective_id=0, has_side_effects=True, vmem_limit_bytes=60 * 2**20
        ),
    )(order, x, q, k, v, o)


def per_device(
    layer_input,
    query_rows,
    key_rows,
    value_rows,
    out_grad,
    block_order,
    master,
    moment_one,
    moment_two,
):
    grad_local = fused(
        block_order, layer_input[0], query_rows[0], key_rows[0], value_rows[0], out_grad[0]
    )
    new_one = BETA_ONE * moment_one + (1.0 - BETA_ONE) * grad_local
    new_two = BETA_TWO * moment_two + (1.0 - BETA_TWO) * grad_local * grad_local
    corr_one = 1.0 - BETA_ONE**STEP
    corr_two = 1.0 - BETA_TWO**STEP
    update = new_one / corr_one / (jnp.sqrt(new_two / corr_two) + EPSILON)
    new_master = master - LEARN_RATE * (update + DECAY * master)
    return (new_master, new_one, new_two)


def solution(mesh):
    rows = P("dp", "ctx", None)
    owned = P(("dp", "ctx"), None)
    return jax.shard_map(
        per_device,
        mesh=mesh,
        in_specs=(rows, rows, rows, rows, rows, P(), owned, owned, owned),
        out_specs=(owned, owned, owned),
        check_vma=False,
    )
```

```python
import functools
import math

import jax
import jax.numpy as jnp
from jax import lax
from jax.experimental import pallas as pl
from jax.experimental.pallas import tpu as pltpu
from jax.sharding import PartitionSpec as P

STEP = 10
NEG_FILL = -1e30
BETA_ONE = 0.9
BETA_TWO = 0.95
EPSILON = 1e-08
LEARN_RATE = 0.01
DECAY = 0.1

F32 = jnp.float32
BF16 = jnp.bfloat16
MESH = pl.DeviceIdType.MESH
ROW_CONTRACT = (((1,), (1,)), ((), ()))

TOK = 128
HD = 128
HALF = 64
NXY = 16
NCTX = 32
NZ = 8
CHUNK = 256
NCHUNK = 5
KEYS = NXY * TOK
KT = 256
SIDE = 256
LOG2E = math.log2(math.e)
OWN = 64
ROWS = 1024
SCALE = 1.0 / math.sqrt(HD)


def fused_kernel(
    order_ref,
    x_hbm,
    q_ref,
    k_ref,
    v_ref,
    o_ref,
    grad_ref,
    kv_all,
    k_t,
    x_mid,
    x_recv,
    x_t,
    s_scr,
    d_scr,
    dkv_acc,
    dkv_send,
    dkv_one,
    dkv_sum,
    dkv_two,
    qo_all,
    st_send,
    st_recv,
    dq_own,
    dq_send,
    dq_recv,
    g_all,
    core_send,
    core_recv,
    half_own,
    z_send,
    z_recv,
    qo_ss,
    qo_rs,
    st_ss,
    st_rs,
    dq_ss,
    dq_rs,
    kv1_ss,
    kv1_rs,
    kv2_ss,
    kv2_rs,
    x0_ss,
    x1_ss,
    x1_rs,
    x2_ss,
    x_rs,
    x_own_sem,
    g1_ss,
    g1_rs,
    g2_ss,
    g2_rs,
    dkv1_ss,
    dkv1_rs,
    dkv2_ss,
    dkv2_rs,
    core_ss,
    core_rs,
    z_ss,
    z_rs,
):
    dp = lax.axis_index("dp")
    ctx = lax.axis_index("ctx")
    core = lax.rem(dp, 2)
    z_lo = dp // 2
    z_hi = lax.rem(ctx, 2)
    plane = ctx // 2
    y = plane // 4
    x = lax.rem(plane, 4)
    z_me = z_hi * 4 + z_lo

    def plane_peer(d):
        return lax.rem(y + d // 4, 4) * 4 + lax.rem(x + lax.rem(d, 4), 4)

    def plane_dev(k):
        return (dp, k * 2 + z_hi)

    def z_peer(d):
        return lax.rem(z_me + d, NZ)

    def z_dev(z):
        return (lax.rem(z, 4) * 2 + core, plane * 2 + z // 4)

    zh_dev = (dp, plane * 2 + (1 - z_hi))
    place = (y, x)

    def line_dev(axis, i):
        return plane_dev(i * 4 + x if axis == 0 else y * 4 + i)

    def line_peer(axis, d):
        return lax.rem(place[axis] + d, 4)

    def remote(src, dst, ss, rs, target):
        return pltpu.make_async_remote_copy(
            src_ref=src,
            dst_ref=dst,
            send_sem=ss,
            recv_sem=rs,
            device_id=target,
            device_id_type=MESH,
        )

    def across(array, half, i):
        return array.at[half, :, i] if half == 0 else array.at[half, i]

    core_dev = (z_lo * 2 + (1 - core), ctx)

    barrier = pltpu.get_barrier_semaphore()

    @pl.loop(1, NXY)
    def _(d):
        pl.semaphore_signal(barrier, inc=1, device_id=plane_dev(plane_peer(d)), device_id_type=MESH)

    @pl.loop(1, NZ)
    def _(d):
        pl.semaphore_signal(barrier, inc=1, device_id=z_dev(z_peer(d)), device_id_type=MESH)

    pl.semaphore_signal(barrier, inc=1, device_id=core_dev, device_id_type=MESH)

    def rows(first, count):
        return pl.ds(pl.multiple_of(first, count), count)

    kv_all[0, y, x] = k_ref[...]
    kv_all[1, y, x] = v_ref[...]
    for c in range(4):
        for i in range(2):
            head = slice((2 * c + i) * HD, (2 * c + i + 1) * HD)
            qo_all[c, 0, 0, i * TOK : (i + 1) * TOK] = q_ref[:, head]
            qo_all[c, 1, 0, i * TOK : (i + 1) * TOK] = o_ref[:, head]

    pl.semaphore_wait(barrier, NXY - 1 + NZ - 1 + 1)

    def qo_copy(c):
        return remote(
            qo_all.at[c, :, 0], qo_all.at[c, :, 1], qo_ss.at[c], qo_rs.at[c], zh_dev
        )

    def st_copy(c):
        return remote(st_send.at[c], st_recv.at[c], st_ss.at[c], st_rs.at[c], zh_dev)

    def dq_copy(c):
        return remote(dq_send.at[c], dq_recv.at[c], dq_ss.at[c], dq_rs.at[c], zh_dev)

    def kv_one(half, d):
        piece = kv_all.at[half, y, x]
        return remote(
            piece,
            piece,
            kv1_ss.at[half, d],
            kv1_rs.at[half, place[half]],
            line_dev(half, line_peer(half, d)),
        )

    def kv_one_arrived(half, d):
        i = line_peer(half, d)
        piece = kv_all.at[half, i, x] if half == 0 else kv_all.at[half, y, i]
        return remote(piece, piece, kv1_ss.at[half, d], kv1_rs.at[half, i], line_dev(half, i))

    def kv_two(half, d):
        axis = 1 - half
        piece = across(kv_all, half, place[axis])
        return remote(
            piece,
            piece,
            kv2_ss.at[half, d],
            kv2_rs.at[half, place[axis]],
            line_dev(axis, line_peer(axis, d)),
        )

    def kv_two_arrived(half, d):
        axis = 1 - half
        i = line_peer(axis, d)
        piece = across(kv_all, half, i)
        return remote(piece, piece, kv2_ss.at[half, d], kv2_rs.at[half, i], line_dev(axis, i))

    def x_columns(half, low, row, col):
        first = (low * 2 + half) * (NCTX * OWN) + (row * 4 + col) * TOK
        return x_hbm.at[:, rows(first, TOK)]

    def x_start(half, d):
        i = line_peer(half, d)
        for e in range(4):
            j = lax.rem(place[1 - half] + e, 4)
            for low in range(4):
                target = x_recv.at[half, y, x, low] if e == 0 else x_mid.at[half, place[half], j, low]
                remote(
                    x_columns(half, low, i, j) if half == 0 else x_columns(half, low, j, i),
                    target,
                    x1_ss.at[half, d],
                    x_rs.at[half, y, x] if e == 0 else x1_rs.at[half, place[half], j],
                    line_dev(half, i),
                ).start()

    def x_start_line(half, d):
        axis = 1 - half
        i = line_peer(axis, d)
        for low in range(4):
            remote(
                x_columns(half, low, y, i) if half == 0 else x_columns(half, low, i, x),
                x_recv.at[half, y, x, low],
                x0_ss.at[half, d],
                x_rs.at[half, y, x],
                line_dev(axis, i),
            ).start()

    def x_own(half, low):
        return pltpu.make_async_copy(
            x_columns(half, low, y, x), x_recv.at[half, y, x, low], x_own_sem.at[half, low]
        )

    def x_two(half, d, e):
        axis = 1 - half
        i = line_peer(half, d)
        j = line_peer(axis, e)
        where = (i, x) if half == 0 else (y, i)
        return remote(
            x_mid.at[half, i, j],
            x_recv.at[half, where[0], where[1]],
            x2_ss.at[half, d, e],
            x_rs.at[half, where[0], where[1]],
            line_dev(axis, j),
        )

    def x_forward(half):
        for d in (1, 3, 2):
            i = line_peer(half, d)
            for e in (1, 3, 2):
                j = line_peer(1 - half, e)
                piece = x_mid.at[half, i, j]
                pltpu.make_async_copy(piece, piece, x1_rs.at[half, i, j]).wait()
                x_two(half, d, e).start()

    steps = [(half, d) for d in (1, 3, 2) for half in (0, 1)]
    for half, d in steps:
        kv_one(half, d).start()
    for c in range(4):
        qo_copy(c).start()
    for half in (0, 1):
        for d in (1, 3, 2):
            kv_one_arrived(half, d).wait_recv()
        for d in (1, 3, 2):
            kv_two(half, d).start()
    x_start(0, 1)
    x_start(1, 1)
    x_start(0, 3)
    x_start(1, 3)
    x_start(0, 2)
    x_start(1, 2)
    x_start_line(0, 1)
    x_start_line(1, 1)
    x_start_line(0, 3)
    x_start_line(1, 3)
    x_start_line(0, 2)
    x_start_line(1, 2)
    for half in (0, 1):
        for low in range(4):
            x_own(half, low).start()
    for half, d in steps:
        kv_two_arrived(half, d).wait_recv()

    lane = lax.broadcasted_iota(jnp.int32, (1, 2 * SIDE), 1)
    token = lax.rem(lane, TOK)
    other = plane * 2 + 1 - z_hi
    first_pos = jnp.where(lane < SIDE, order_ref[2 * ctx], order_ref[2 * other])
    second_pos = jnp.where(lane < SIDE, order_ref[2 * ctx + 1], order_ref[2 * other + 1])
    query_pos = jnp.where(token < HALF, first_pos, second_pos) * HALF + lax.rem(token, HALF)
    sub = lax.broadcasted_iota(jnp.int32, (HALF, 2 * SIDE), 0)

    @pl.loop(0, NXY)
    def _(b):
        k_t[:, rows(b * TOK, TOK)] = kv_all[0, b // 4, lax.rem(b, 4)].T

    def g_one(chunk, half, d):
        piece = g_all.at[chunk, half, y, x]
        return remote(
            piece,
            piece,
            g1_ss.at[chunk, half, d],
            g1_rs.at[chunk, half, place[half]],
            line_dev(half, line_peer(half, d)),
        )

    def g_one_arrived(chunk, half, d):
        i = line_peer(half, d)
        piece = g_all.at[chunk, half, i, x] if half == 0 else g_all.at[chunk, half, y, i]
        return remote(
            piece, piece, g1_ss.at[chunk, half, d], g1_rs.at[chunk, half, i], line_dev(half, i)
        )

    def g_two(chunk, half, d):
        axis = 1 - half
        piece = across(g_all.at[chunk], half, place[axis])
        return remote(
            piece,
            piece,
            g2_ss.at[chunk, half, d],
            g2_rs.at[chunk, half, place[axis]],
            line_dev(axis, line_peer(axis, d)),
        )

    def g_two_arrived(chunk, half, d):
        axis = 1 - half
        i = line_peer(axis, d)
        piece = across(g_all.at[chunk], half, i)
        return remote(
            piece, piece, g2_ss.at[chunk, half, d], g2_rs.at[chunk, half, i], line_dev(axis, i)
        )

    def send_chunk(chunk):
        for half, d in steps:
            g_one(chunk, half, d).start()

    def forward_chunk(chunk):
        for half in (0, 1):
            for d in (1, 3, 2):
                g_one_arrived(chunk, half, d).wait_recv()
            for d in (1, 3, 2):
                g_two(chunk, half, d).start()

    def dkv_first(half, d):
        i = line_peer(half, d)
        return remote(
            dkv_send.at[half, i] if half == 0 else dkv_send.at[half, :, i],
            dkv_one.at[half, place[half]],
            dkv1_ss.at[half, d],
            dkv1_rs.at[half, place[half]],
            line_dev(half, i),
        )

    def dkv_first_arrived(half, d):
        i = line_peer(half, d)
        return remote(
            dkv_one.at[half, i],
            dkv_one.at[half, i],
            dkv1_ss.at[half, d],
            dkv1_rs.at[half, i],
            line_dev(half, i),
        )

    def dkv_second(half, d):
        axis = 1 - half
        i = line_peer(axis, d)
        return remote(
            dkv_sum.at[half, i],
            dkv_two.at[half, place[axis]],
            dkv2_ss.at[half, d],
            dkv2_rs.at[half, place[axis]],
            line_dev(axis, i),
        )

    def dkv_second_arrived(half, d):
        axis = 1 - half
        i = line_peer(axis, d)
        return remote(
            dkv_two.at[half, i],
            dkv_two.at[half, i],
            dkv2_ss.at[half, d],
            dkv2_rs.at[half, i],
            line_dev(axis, i),
        )

    def key_tile(ref, half, t):
        return ref.at[half, t // 2, pl.ds(lax.rem(t, 2) * 2, 2)]

    def fold(a, op):
        return op(a.reshape(a.shape[0] // 8, 8, a.shape[1]), axis=0)

    def local_pass(c):
        slot = c % 2
        q_c = qo_all[c, 0].reshape(2 * SIDE, HD)
        o_c = qo_all[c, 1].reshape(2 * SIDE, HD)

        def scores_tile(t, top):
            first = pl.multiple_of(t * KT, KT)
            s = lax.dot_general(
                key_tile(kv_all, 0, t)[...].reshape(KT, HD),
                q_c,
                ROW_CONTRACT,
                preferred_element_type=F32,
            )
            d_scr[slot, pl.ds(first, KT)] = lax.dot_general(
                key_tile(kv_all, 1, t)[...].reshape(KT, HD),
                o_c,
                ROW_CONTRACT,
                preferred_element_type=F32,
            )
            for b in range(KT // HALF):
                owner = (t * 2 + b // 2) * 2 + z_hi
                limit = query_pos - order_ref[owner * 2 + b % 2] * HALF
                part = jnp.where(sub <= limit, s[b * HALF : (b + 1) * HALF], NEG_FILL)
                s_scr[slot, pl.ds(first + b * HALF, HALF)] = part
                top = jnp.maximum(top, fold(part, jnp.max))
            return top

        top = lax.fori_loop(0, KEYS // KT, scores_tile, jnp.full((8, 2 * SIDE), NEG_FILL, F32))
        top = jnp.max(top, axis=0, keepdims=True)

        def weights_tile(t, carried):
            total, inner = carried
            tile = pl.ds(pl.multiple_of(t * KT, KT), KT)
            e = jnp.exp2((s_scr[slot, tile] - top) * (SCALE * LOG2E))
            s_scr[slot, tile] = e
            return total + fold(e, jnp.sum), inner + fold(e * d_scr[slot, tile], jnp.sum)

        zero = jnp.zeros((8, 2 * SIDE), F32)
        total, inner = lax.fori_loop(0, KEYS // KT, weights_tile, (zero, zero))
        st_send[c, 0:8] = jnp.broadcast_to(top, (8, 2 * SIDE))
        st_send[c, 8:16] = jnp.broadcast_to(jnp.sum(total, axis=0, keepdims=True), (8, 2 * SIDE))
        st_send[c, 16:24] = jnp.broadcast_to(jnp.sum(inner, axis=0, keepdims=True), (8, 2 * SIDE))
        st_copy(c).start()

    def gradient_pass(c):
        slot = c % 2
        q_c = qo_all[c, 0].reshape(2 * SIDE, HD)
        o_c = qo_all[c, 1].reshape(2 * SIDE, HD)
        st_copy(c).wait_recv()

        def theirs(first):
            return jnp.concatenate(
                [
                    st_recv[c, first : first + 8, SIDE:],
                    st_recv[c, first : first + 8, :SIDE],
                ],
                axis=1,
            )

        mine_top = st_send[c, 0:8]
        top = jnp.maximum(mine_top, theirs(0))
        mine = jnp.exp2((mine_top - top) * (SCALE * LOG2E))
        other_part = jnp.exp2((theirs(0) - top) * (SCALE * LOG2E))
        whole = 1.0 / (st_send[c, 8:16] * mine + theirs(8) * other_part)
        delta = ((st_send[c, 16:24] * mine + theirs(16) * other_part) * whole)[:1]
        inv = (mine * whole)[:1]

        def grads_tile(t, dq):
            tile = pl.ds(pl.multiple_of(t * KT, KT), KT)
            p = s_scr[slot, tile] * inv
            ds = (p * (d_scr[slot, tile] - delta) * SCALE).astype(BF16)
            dk = jnp.dot(ds, q_c, preferred_element_type=F32)
            dv = jnp.dot(p.astype(BF16), o_c, preferred_element_type=F32)
            if c == 0:
                dkv_acc[tile, :HD] = dk
                dkv_acc[tile, HD:] = dv
            elif c < 3:
                dkv_acc[tile, :HD] += dk
                dkv_acc[tile, HD:] += dv
            else:
                dk = (dkv_acc[tile, :HD] + dk).astype(BF16)
                dv = (dkv_acc[tile, HD:] + dv).astype(BF16)
                key_tile(dkv_send, 0, t)[...] = dk.reshape(2, TOK, HD)
                key_tile(dkv_send, 1, t)[...] = dv.reshape(2, TOK, HD)
            return dq + jnp.dot(k_t[:, tile], ds, preferred_element_type=F32)

        dq = lax.fori_loop(0, KEYS // KT, grads_tile, jnp.zeros((HD, 2 * SIDE), F32))
        dq_own[c] = dq[:, :SIDE]
        dq_send[c] = dq[:, SIDE:]
        dq_copy(c).start()

    def finish_queries(c):
        dq_copy(c).wait_recv()
        for i in range(2):
            part = slice(i * TOK, (i + 1) * TOK)
            g_all[c, i, y, x] = (dq_own[c, :, part] + dq_recv[c, :, part]).T.astype(BF16)
        send_chunk(c)

    for c in range(4):
        qo_copy(c).wait_recv()
        local_pass(c)
        if c > 0:
            gradient_pass(c - 1)
        if c == 2:
            x_forward(0)
            x_forward(1)
        if c > 1:
            finish_queries(c - 2)
        if c > 2:
            forward_chunk(c - 3)
    gradient_pass(3)
    for half, d in steps:
        dkv_first(half, d).start()
    finish_queries(2)
    forward_chunk(1)
    finish_queries(3)
    forward_chunk(2)

    for half in (0, 1):
        for d in (1, 3, 2):
            dkv_first_arrived(half, d).wait_recv()
        for j in range(4):
            piece = dkv_send[half, y, j] if half == 0 else dkv_send[half, j, x]
            total = piece.astype(F32)
            for d in (1, 3, 2):
                total += dkv_one[half, line_peer(half, d), j].astype(F32)
            dkv_sum[half, j] = total
        for d in (1, 3, 2):
            dkv_second(half, d).start()

    forward_chunk(3)

    for half in (0, 1):
        axis = 1 - half
        total = dkv_sum[half, place[axis]]
        for d in (1, 3, 2):
            dkv_second_arrived(half, d).wait_recv()
            total += dkv_two[half, line_peer(axis, d)]
        g_all[4, half, y, x] = total.astype(BF16)
    send_chunk(4)

    def transpose_slot(row, col):
        for half in (0, 1):
            for low in range(4):
                first = (half * 4 + low) * TOK
                x_t[first : first + TOK, rows((row * 4 + col) * TOK, TOK)] = x_recv[
                    half, row, col, low
                ].T

    for half in (0, 1):
        for low in range(4):
            x_own(half, low).wait()
    transpose_slot(y, x)

    @pl.loop(1, NXY)
    def _(d):
        k = plane_peer(d)
        row, col = k // 4, lax.rem(k, 4)
        for half in (0, 1):
            piece = x_recv.at[half, row, col]
            pltpu.make_async_copy(piece, piece, x_rs.at[half, row, col]).wait()
        transpose_slot(row, col)

    def z_copy(chunk, z, d):
        return remote(
            z_send.at[chunk, z],
            z_recv.at[chunk, z_me],
            z_ss.at[chunk, d],
            z_rs.at[chunk, z_me],
            z_dev(z),
        )

    def z_arrived(chunk, z):
        return remote(
            z_send.at[chunk, z],
            z_recv.at[chunk, z],
            z_ss.at[chunk, 0],
            z_rs.at[chunk, z],
            z_dev(z),
        )

    def core_copy(chunk):
        return remote(
            core_send.at[chunk],
            core_recv.at[chunk],
            core_ss.at[chunk],
            core_rs.at[chunk],
            core_dev,
        )

    def multiply(c):
        for half, d in steps:
            g_two_arrived(c, half, d).wait_recv()
        columns = jnp.concatenate(
            [g_all[c, half].reshape(NXY * TOK, HD) for half in (0, 1)], axis=1
        )

        def product(first):
            return jnp.dot(
                x_t[pl.ds(pl.multiple_of(first, 256), 256)], columns, preferred_element_type=F32
            )

        @pl.loop(0, 2)
        def _(i):
            core_send[c, rows(i * 256, 256)] = product((1 - core) * 512 + i * 256)

        core_copy(c).start()

        @pl.loop(0, 2)
        def _(i):
            half_own[c, rows(i * 256, 256)] = product(core * 512 + i * 256)

    def reduce_cores(c):
        core_copy(c).wait_recv()
        for j in range(NZ):
            z = (j % 2) * 4 + j // 2
            part = pl.ds(j * OWN, OWN)
            total = half_own[c, part] + core_recv[c, part]
            half_own[c, part] = total
            z_send[c, z] = total.astype(BF16)

        @pl.loop(1, NZ)
        def _(d):
            z_copy(c, z_peer(d), d).start()

    multiply(0)
    multiply(1)
    reduce_cores(0)
    reduce_cores(1)
    multiply(2)
    forward_chunk(4)
    multiply(3)
    reduce_cores(2)
    reduce_cores(3)
    multiply(4)
    reduce_cores(4)

    for c in range(NCHUNK):
        def add_slot(d, total):
            z = z_peer(d)
            z_arrived(c, z).wait_recv()
            return total + z_recv[c, z].astype(F32)

        own_part = half_own[c, rows((z_lo * 2 + z_hi) * OWN, OWN)]
        grad_ref[:, c * CHUNK : (c + 1) * CHUNK] = lax.fori_loop(1, NZ, add_slot, own_part)

    for c in range(4):
        qo_copy(c).wait_send()
        st_copy(c).wait_send()
        dq_copy(c).wait_send()
    for half, d in steps:
        kv_one(half, d).wait_send()
        kv_two(half, d).wait_send()
        dkv_first(half, d).wait_send()
        dkv_second(half, d).wait_send()
        for c in range(NCHUNK):
            g_one(c, half, d).wait_send()
            g_two(c, half, d).wait_send()
        pltpu.make_async_copy(x_mid.at[0, 0], x_mid.at[0, 0], x1_ss.at[half, d]).wait()
        pltpu.make_async_copy(x_recv.at[0, 0, 0], x_recv.at[0, 0, 0], x0_ss.at[half, d]).wait()
        for e in (1, 2, 3):
            x_two(half, d, e).wait_send()

    for c in range(NCHUNK):
        core_copy(c).wait_send()

        @pl.loop(1, NZ)
        def _(d):
            z_copy(c, z_peer(d), d).wait_send()


def fused(order, x, q, k, v, o):
    vmem = pl.BlockSpec(memory_space=pltpu.VMEM)
    dma = pltpu.SemaphoreType.DMA
    scratch = [
        pltpu.VMEM((2, 4, 4, TOK, HD), BF16),
        pltpu.VMEM((HD, KEYS), BF16),
        pltpu.VMEM((2, 4, 4, 4, TOK, TOK), BF16),
        pltpu.VMEM((2, 4, 4, 4, TOK, TOK), BF16),
        pltpu.VMEM((ROWS, NXY * TOK), BF16),
        pltpu.VMEM((2, KEYS, 2 * SIDE), F32),
        pltpu.VMEM((2, KEYS, 2 * SIDE), F32),
        pltpu.VMEM((KEYS, 2 * HD), F32),
        pltpu.VMEM((2, 4, 4, TOK, HD), BF16),
        pltpu.VMEM((2, 4, 4, TOK, HD), BF16),
        pltpu.VMEM((2, 4, TOK, HD), F32),
        pltpu.VMEM((2, 4, TOK, HD), F32),
        pltpu.VMEM((4, 2, 2, SIDE, HD), BF16),
        pltpu.VMEM((4, 24, 2 * SIDE), F32),
        pltpu.VMEM((4, 24, 2 * SIDE), F32),
        pltpu.VMEM((4, HD, SIDE), F32),
        pltpu.VMEM((4, HD, SIDE), F32),
        pltpu.VMEM((4, HD, SIDE), F32),
        pltpu.VMEM((NCHUNK, 2, 4, 4, TOK, HD), BF16),
        pltpu.VMEM((NCHUNK, ROWS // 2, CHUNK), F32),
        pltpu.VMEM((NCHUNK, ROWS // 2, CHUNK), F32),
        pltpu.VMEM((NCHUNK, ROWS // 2, CHUNK), F32),
        pltpu.VMEM((NCHUNK, NZ, OWN, CHUNK), BF16),
        pltpu.VMEM((NCHUNK, NZ, OWN, CHUNK), BF16),
        dma((4,)),
        dma((4,)),
        dma((4,)),
        dma((4,)),
        dma((4,)),
        dma((4,)),
        dma((2, 4)),
        dma((2, 4)),
        dma((2, 4)),
        dma((2, 4)),
        dma((2, 4)),
        dma((2, 4)),
        dma((2, 4, 4)),
        dma((2, 4, 4)),
        dma((2, 4, 4)),
        dma((2, 4)),
        dma((NCHUNK, 2, 4)),
        dma((NCHUNK, 2, 4)),
        dma((NCHUNK, 2, 4)),
        dma((NCHUNK, 2, 4)),
        dma((2, 4)),
        dma((2, 4)),
        dma((2, 4)),
        dma((2, 4)),
        dma((NCHUNK,)),
        dma((NCHUNK,)),
        dma((NCHUNK, NZ)),
        dma((NCHUNK, NZ)),
    ]
    return pl.pallas_call(
        fused_kernel,
        name="attention_backward_and_weight_gradient",
        out_shape=jax.ShapeDtypeStruct((OWN, NCHUNK * CHUNK), F32),
        in_specs=[
            pl.BlockSpec(memory_space=pltpu.SMEM),
            pl.BlockSpec(memory_space=pl.ANY),
            vmem,
            vmem,
            vmem,
            vmem,
        ],
        out_specs=vmem,
        scratch_shapes=scratch,
        compiler_params=pltpu.CompilerParams(
            collective_id=0, has_side_effects=True, vmem_limit_bytes=60 * 2**20
        ),
    )(order, x, q, k, v, o)


def per_device(
    layer_input,
    query_rows,
    key_rows,
    value_rows,
    out_grad,
    block_order,
    master,
    moment_one,
    moment_two,
):
    grad_local = fused(
        block_order, layer_input[0], query_rows[0], key_rows[0], value_rows[0], out_grad[0]
    )
    new_one = BETA_ONE * moment_one + (1.0 - BETA_ONE) * grad_local
    new_two = BETA_TWO * moment_two + (1.0 - BETA_TWO) * grad_local * grad_local
    corr_one = 1.0 - BETA_ONE**STEP
    corr_two = 1.0 - BETA_TWO**STEP
    update = new_one / corr_one / (jnp.sqrt(new_two / corr_two) + EPSILON)
    new_master = master - LEARN_RATE * (update + DECAY * master)
    return (new_master, new_one, new_two)


def solution(mesh):
    rows = P("dp", "ctx", None)
    owned = P(("dp", "ctx"), None)
    return jax.shard_map(
        per_device,
        mesh=mesh,
        in_specs=(rows, rows, rows, rows, rows, P(), owned, owned, owned),
        out_specs=(owned, owned, owned),
        check_vma=False,
    )
```

```python
import functools
import math

import jax
import jax.numpy as jnp
from jax import lax
from jax.experimental import pallas as pl
from jax.experimental.pallas import tpu as pltpu
from jax.sharding import PartitionSpec as P

STEP = 10
NEG_FILL = -1e30
BETA_ONE = 0.9
BETA_TWO = 0.95
EPSILON = 1e-08
LEARN_RATE = 0.01
DECAY = 0.1

F32 = jnp.float32
BF16 = jnp.bfloat16
MESH = pl.DeviceIdType.MESH
ROW_CONTRACT = (((1,), (1,)), ((), ()))

TOK = 128
HD = 128
HALF = 64
NXY = 16
NCTX = 32
NZ = 8
CHUNK = 256
NCHUNK = 5
KEYS = NXY * TOK
KT = 256
SIDE = 256
LOG2E = math.log2(math.e)
OWN = 64
ROWS = 1024
SCALE = 1.0 / math.sqrt(HD)


def fused_kernel(
    order_ref,
    x_hbm,
    q_ref,
    k_ref,
    v_ref,
    o_ref,
    grad_ref,
    kv_all,
    k_t,
    x_mid,
    x_recv,
    x_t,
    s_scr,
    d_scr,
    dkv_acc,
    dkv_send,
    dkv_one,
    dkv_sum,
    dkv_two,
    qo_all,
    st_send,
    st_recv,
    dq_own,
    dq_send,
    dq_recv,
    g_all,
    core_send,
    core_recv,
    half_own,
    z_send,
    z_recv,
    qo_ss,
    qo_rs,
    st_ss,
    st_rs,
    dq_ss,
    dq_rs,
    kv1_ss,
    kv1_rs,
    kv2_ss,
    kv2_rs,
    x0_ss,
    x1_ss,
    x1_rs,
    x2_ss,
    x_rs,
    x_own_sem,
    g1_ss,
    g1_rs,
    g2_ss,
    g2_rs,
    dkv1_ss,
    dkv1_rs,
    dkv2_ss,
    dkv2_rs,
    core_ss,
    core_rs,
    z_ss,
    z_rs,
):
    dp = lax.axis_index("dp")
    ctx = lax.axis_index("ctx")
    core = lax.rem(dp, 2)
    z_lo = dp // 2
    z_hi = lax.rem(ctx, 2)
    plane = ctx // 2
    y = plane // 4
    x = lax.rem(plane, 4)
    z_me = z_hi * 4 + z_lo

    def plane_peer(d):
        return lax.rem(y + d // 4, 4) * 4 + lax.rem(x + lax.rem(d, 4), 4)

    def plane_dev(k):
        return (dp, k * 2 + z_hi)

    def z_peer(d):
        return lax.rem(z_me + d, NZ)

    def z_dev(z):
        return (lax.rem(z, 4) * 2 + core, plane * 2 + z // 4)

    zh_dev = (dp, plane * 2 + (1 - z_hi))
    place = (y, x)

    def line_dev(axis, i):
        return plane_dev(i * 4 + x if axis == 0 else y * 4 + i)

    def line_peer(axis, d):
        return lax.rem(place[axis] + d, 4)

    def remote(src, dst, ss, rs, target):
        return pltpu.make_async_remote_copy(
            src_ref=src,
            dst_ref=dst,
            send_sem=ss,
            recv_sem=rs,
            device_id=target,
            device_id_type=MESH,
        )

    def across(array, half, i):
        return array.at[half, :, i] if half == 0 else array.at[half, i]

    core_dev = (z_lo * 2 + (1 - core), ctx)

    barrier = pltpu.get_barrier_semaphore()

    @pl.loop(1, NXY)
    def _(d):
        pl.semaphore_signal(barrier, inc=1, device_id=plane_dev(plane_peer(d)), device_id_type=MESH)

    @pl.loop(1, NZ)
    def _(d):
        pl.semaphore_signal(barrier, inc=1, device_id=z_dev(z_peer(d)), device_id_type=MESH)

    pl.semaphore_signal(barrier, inc=1, device_id=core_dev, device_id_type=MESH)

    def rows(first, count):
        return pl.ds(pl.multiple_of(first, count), count)

    kv_all[0, y, x] = k_ref[...]
    kv_all[1, y, x] = v_ref[...]
    for c in range(4):
        for i in range(2):
            head = slice((2 * c + i) * HD, (2 * c + i + 1) * HD)
            qo_all[c, 0, 0, i * TOK : (i + 1) * TOK] = q_ref[:, head]
            qo_all[c, 1, 0, i * TOK : (i + 1) * TOK] = o_ref[:, head]

    pl.semaphore_wait(barrier, NXY - 1 + NZ - 1 + 1)

    def qo_copy(c):
        return remote(
            qo_all.at[c, :, 0], qo_all.at[c, :, 1], qo_ss.at[c], qo_rs.at[c], zh_dev
        )

    def st_copy(c):
        return remote(st_send.at[c], st_recv.at[c], st_ss.at[c], st_rs.at[c], zh_dev)

    def dq_copy(c):
        return remote(dq_send.at[c], dq_recv.at[c], dq_ss.at[c], dq_rs.at[c], zh_dev)

    def kv_one(half, d):
        piece = kv_all.at[half, y, x]
        return remote(
            piece,
            piece,
            kv1_ss.at[half, d],
            kv1_rs.at[half, place[half]],
            line_dev(half, line_peer(half, d)),
        )

    def kv_one_arrived(half, d):
        i = line_peer(half, d)
        piece = kv_all.at[half, i, x] if half == 0 else kv_all.at[half, y, i]
        return remote(piece, piece, kv1_ss.at[half, d], kv1_rs.at[half, i], line_dev(half, i))

    def kv_two(half, d):
        axis = 1 - half
        piece = across(kv_all, half, place[axis])
        return remote(
            piece,
            piece,
            kv2_ss.at[half, d],
            kv2_rs.at[half, place[axis]],
            line_dev(axis, line_peer(axis, d)),
        )

    def kv_two_arrived(half, d):
        axis = 1 - half
        i = line_peer(axis, d)
        piece = across(kv_all, half, i)
        return remote(piece, piece, kv2_ss.at[half, d], kv2_rs.at[half, i], line_dev(axis, i))

    def x_columns(half, low, row, col):
        first = (low * 2 + half) * (NCTX * OWN) + (row * 4 + col) * TOK
        return x_hbm.at[:, rows(first, TOK)]

    def x_start(half, d):
        i = line_peer(half, d)
        for e in range(4):
            j = lax.rem(place[1 - half] + e, 4)
            for low in range(4):
                target = x_recv.at[half, y, x, low] if e == 0 else x_mid.at[half, place[half], j, low]
                remote(
                    x_columns(half, low, i, j) if half == 0 else x_columns(half, low, j, i),
                    target,
                    x1_ss.at[half, d],
                    x_rs.at[half, y, x] if e == 0 else x1_rs.at[half, place[half], j],
                    line_dev(half, i),
                ).start()

    def x_start_line(half, d):
        axis = 1 - half
        i = line_peer(axis, d)
        for low in range(4):
            remote(
                x_columns(half, low, y, i) if half == 0 else x_columns(half, low, i, x),
                x_recv.at[half, y, x, low],
                x0_ss.at[half, d],
                x_rs.at[half, y, x],
                line_dev(axis, i),
            ).start()

    def x_own(half, low):
        return pltpu.make_async_copy(
            x_columns(half, low, y, x), x_recv.at[half, y, x, low], x_own_sem.at[half, low]
        )

    def x_two(half, d, e):
        axis = 1 - half
        i = line_peer(half, d)
        j = line_peer(axis, e)
        where = (i, x) if half == 0 else (y, i)
        return remote(
            x_mid.at[half, i, j],
            x_recv.at[half, where[0], where[1]],
            x2_ss.at[half, d, e],
            x_rs.at[half, where[0], where[1]],
            line_dev(axis, j),
        )

    def x_forward(half):
        for d in (1, 3, 2):
            i = line_peer(half, d)
            for e in (1, 3, 2):
                j = line_peer(1 - half, e)
                piece = x_mid.at[half, i, j]
                pltpu.make_async_copy(piece, piece, x1_rs.at[half, i, j]).wait()
                x_two(half, d, e).start()

    steps = [(half, d) for d in (1, 3, 2) for half in (0, 1)]
    for half, d in steps:
        kv_one(half, d).start()
    for c in range(4):
        qo_copy(c).start()
    for half in (0, 1):
        for d in (1, 3, 2):
            kv_one_arrived(half, d).wait_recv()
        for d in (1, 3, 2):
            kv_two(half, d).start()
    x_start(0, 1)
    x_start(1, 1)
    x_start(0, 3)
    x_start(1, 3)
    x_start(0, 2)
    x_start(1, 2)
    x_start_line(0, 1)
    x_start_line(1, 1)
    x_start_line(0, 3)
    x_start_line(1, 3)
    x_start_line(0, 2)
    x_start_line(1, 2)
    for half in (0, 1):
        for low in range(4):
            x_own(half, low).start()
    for half, d in steps:
        kv_two_arrived(half, d).wait_recv()

    lane = lax.broadcasted_iota(jnp.int32, (1, 2 * SIDE), 1)
    token = lax.rem(lane, TOK)
    other = plane * 2 + 1 - z_hi
    first_pos = jnp.where(lane < SIDE, order_ref[2 * ctx], order_ref[2 * other])
    second_pos = jnp.where(lane < SIDE, order_ref[2 * ctx + 1], order_ref[2 * other + 1])
    query_pos = jnp.where(token < HALF, first_pos, second_pos) * HALF + lax.rem(token, HALF)
    sub = lax.broadcasted_iota(jnp.int32, (HALF, 2 * SIDE), 0)

    @pl.loop(0, NXY)
    def _(b):
        k_t[:, rows(b * TOK, TOK)] = kv_all[0, b // 4, lax.rem(b, 4)].T

    def g_one(chunk, half, d):
        piece = g_all.at[chunk, half, y, x]
        return remote(
            piece,
            piece,
            g1_ss.at[chunk, half, d],
            g1_rs.at[chunk, half, place[half]],
            line_dev(half, line_peer(half, d)),
        )

    def g_one_arrived(chunk, half, d):
        i = line_peer(half, d)
        piece = g_all.at[chunk, half, i, x] if half == 0 else g_all.at[chunk, half, y, i]
        return remote(
            piece, piece, g1_ss.at[chunk, half, d], g1_rs.at[chunk, half, i], line_dev(half, i)
        )

    def g_two(chunk, half, d):
        axis = 1 - half
        piece = across(g_all.at[chunk], half, place[axis])
        return remote(
            piece,
            piece,
            g2_ss.at[chunk, half, d],
            g2_rs.at[chunk, half, place[axis]],
            line_dev(axis, line_peer(axis, d)),
        )

    def g_two_arrived(chunk, half, d):
        axis = 1 - half
        i = line_peer(axis, d)
        piece = across(g_all.at[chunk], half, i)
        return remote(
            piece, piece, g2_ss.at[chunk, half, d], g2_rs.at[chunk, half, i], line_dev(axis, i)
        )

    def send_chunk(chunk):
        for half, d in steps:
            g_one(chunk, half, d).start()

    def forward_chunk(chunk):
        for half in (0, 1):
            for d in (1, 3, 2):
                g_one_arrived(chunk, half, d).wait_recv()
            for d in (1, 3, 2):
                g_two(chunk, half, d).start()

    def dkv_first(half, d):
        i = line_peer(half, d)
        return remote(
            dkv_send.at[half, i] if half == 0 else dkv_send.at[half, :, i],
            dkv_one.at[half, place[half]],
            dkv1_ss.at[half, d],
            dkv1_rs.at[half, place[half]],
            line_dev(half, i),
        )

    def dkv_first_arrived(half, d):
        i = line_peer(half, d)
        return remote(
            dkv_one.at[half, i],
            dkv_one.at[half, i],
            dkv1_ss.at[half, d],
            dkv1_rs.at[half, i],
            line_dev(half, i),
        )

    def dkv_second(half, d):
        axis = 1 - half
        i = line_peer(axis, d)
        return remote(
            dkv_sum.at[half, i],
            dkv_two.at[half, place[axis]],
            dkv2_ss.at[half, d],
            dkv2_rs.at[half, place[axis]],
            line_dev(axis, i),
        )

    def dkv_second_arrived(half, d):
        axis = 1 - half
        i = line_peer(axis, d)
        return remote(
            dkv_two.at[half, i],
            dkv_two.at[half, i],
            dkv2_ss.at[half, d],
            dkv2_rs.at[half, i],
            line_dev(axis, i),
        )

    def key_tile(ref, half, t):
        return ref.at[half, t // 2, pl.ds(lax.rem(t, 2) * 2, 2)]

    def fold(a, op):
        return op(a.reshape(a.shape[0] // 8, 8, a.shape[1]), axis=0)

    def local_pass(c):
        slot = c % 2
        q_c = qo_all[c, 0].reshape(2 * SIDE, HD)
        o_c = qo_all[c, 1].reshape(2 * SIDE, HD)

        def scores_tile(t, top):
            first = pl.multiple_of(t * KT, KT)
            s = lax.dot_general(
                key_tile(kv_all, 0, t)[...].reshape(KT, HD),
                q_c,
                ROW_CONTRACT,
                preferred_element_type=F32,
            )
            d_scr[slot, pl.ds(first, KT)] = lax.dot_general(
                key_tile(kv_all, 1, t)[...].reshape(KT, HD),
                o_c,
                ROW_CONTRACT,
                preferred_element_type=F32,
            )
            for b in range(KT // HALF):
                owner = (t * 2 + b // 2) * 2 + z_hi
                limit = query_pos - order_ref[owner * 2 + b % 2] * HALF
                part = jnp.where(sub <= limit, s[b * HALF : (b + 1) * HALF], NEG_FILL)
                s_scr[slot, pl.ds(first + b * HALF, HALF)] = part
                top = jnp.maximum(top, fold(part, jnp.max))
            return top

        top = lax.fori_loop(0, KEYS // KT, scores_tile, jnp.full((8, 2 * SIDE), NEG_FILL, F32))
        top = jnp.max(top, axis=0, keepdims=True)

        def weights_tile(t, carried):
            total, inner = carried
            tile = pl.ds(pl.multiple_of(t * KT, KT), KT)
            e = jnp.exp2((s_scr[slot, tile] - top) * (SCALE * LOG2E))
            s_scr[slot, tile] = e
            return total + fold(e, jnp.sum), inner + fold(e * d_scr[slot, tile], jnp.sum)

        zero = jnp.zeros((8, 2 * SIDE), F32)
        total, inner = lax.fori_loop(0, KEYS // KT, weights_tile, (zero, zero))
        row = lax.broadcasted_iota(jnp.int32, (8, 2 * SIDE), 0)
        total = jnp.sum(total, axis=0, keepdims=True)
        inner = jnp.sum(inner, axis=0, keepdims=True)
        st_send[c] = jnp.where(row == 0, top, jnp.where(row == 1, total, inner))
        st_copy(c).start()

    def gradient_pass(c):
        slot = c % 2
        q_c = qo_all[c, 0].reshape(2 * SIDE, HD)
        o_c = qo_all[c, 1].reshape(2 * SIDE, HD)
        st_copy(c).wait_recv()

        mine_top, mine_total, mine_inner = (st_send[c, r : r + 1] for r in range(3))
        their_top, their_total, their_inner = (
            jnp.concatenate([st_recv[c, r : r + 1, SIDE:], st_recv[c, r : r + 1, :SIDE]], axis=1)
            for r in range(3)
        )
        top = jnp.maximum(mine_top, their_top)
        mine = jnp.exp2((mine_top - top) * (SCALE * LOG2E))
        theirs = jnp.exp2((their_top - top) * (SCALE * LOG2E))
        whole = 1.0 / (mine_total * mine + their_total * theirs)
        delta = (mine_inner * mine + their_inner * theirs) * whole
        inv = mine * whole

        def grads_tile(t, dq):
            tile = pl.ds(pl.multiple_of(t * KT, KT), KT)
            p = s_scr[slot, tile] * inv
            ds = (p * (d_scr[slot, tile] - delta) * SCALE).astype(BF16)
            dk = jnp.dot(ds, q_c, preferred_element_type=F32)
            dv = jnp.dot(p.astype(BF16), o_c, preferred_element_type=F32)
            if c == 0:
                dkv_acc[tile, :HD] = dk
                dkv_acc[tile, HD:] = dv
            elif c < 3:
                dkv_acc[tile, :HD] += dk
                dkv_acc[tile, HD:] += dv
            else:
                dk = (dkv_acc[tile, :HD] + dk).astype(BF16)
                dv = (dkv_acc[tile, HD:] + dv).astype(BF16)
                key_tile(dkv_send, 0, t)[...] = dk.reshape(2, TOK, HD)
                key_tile(dkv_send, 1, t)[...] = dv.reshape(2, TOK, HD)
            return dq + jnp.dot(k_t[:, tile], ds, preferred_element_type=F32)

        dq = lax.fori_loop(0, KEYS // KT, grads_tile, jnp.zeros((HD, 2 * SIDE), F32))
        dq_own[c] = dq[:, :SIDE]
        dq_send[c] = dq[:, SIDE:]
        dq_copy(c).start()

    def finish_queries(c):
        dq_copy(c).wait_recv()
        for i in range(2):
            part = slice(i * TOK, (i + 1) * TOK)
            g_all[c, i, y, x] = (dq_own[c, :, part] + dq_recv[c, :, part]).T.astype(BF16)
        send_chunk(c)

    for c in range(4):
        qo_copy(c).wait_recv()
        local_pass(c)
        if c > 0:
            gradient_pass(c - 1)
        if c == 1:
            x_forward(0)
            x_forward(1)
        if c > 1:
            finish_queries(c - 2)
        if c > 2:
            forward_chunk(c - 3)
    gradient_pass(3)
    def sum_first():
        for half in (0, 1):
            for d in (1, 3, 2):
                dkv_first_arrived(half, d).wait_recv()
            for j in range(4):
                piece = dkv_send[half, y, j] if half == 0 else dkv_send[half, j, x]
                total = piece.astype(F32)
                for d in (1, 3, 2):
                    total += dkv_one[half, line_peer(half, d), j].astype(F32)
                dkv_sum[half, j] = total
            for d in (1, 3, 2):
                dkv_second(half, d).start()

    def sum_second():
        for half in (0, 1):
            axis = 1 - half
            total = dkv_sum[half, place[axis]]
            for d in (1, 3, 2):
                dkv_second_arrived(half, d).wait_recv()
                total += dkv_two[half, line_peer(axis, d)]
            g_all[4, half, y, x] = total.astype(BF16)
        send_chunk(4)

    def transpose_slot(row, col):
        for half in (0, 1):
            for low in range(4):
                first = (half * 4 + low) * TOK
                x_t[first : first + TOK, rows((row * 4 + col) * TOK, TOK)] = x_recv[
                    half, row, col, low
                ].T

    def take_input():
        for half in (0, 1):
            for low in range(4):
                x_own(half, low).wait()
        transpose_slot(y, x)

        @pl.loop(1, NXY)
        def _(d):
            k = plane_peer(d)
            row, col = k // 4, lax.rem(k, 4)
            for half in (0, 1):
                piece = x_recv.at[half, row, col]
                pltpu.make_async_copy(piece, piece, x_rs.at[half, row, col]).wait()
            transpose_slot(row, col)

    def z_copy(chunk, z, d):
        return remote(
            z_send.at[chunk, z],
            z_recv.at[chunk, z_me],
            z_ss.at[chunk, d],
            z_rs.at[chunk, z_me],
            z_dev(z),
        )

    def z_arrived(chunk, z):
        return remote(
            z_send.at[chunk, z],
            z_recv.at[chunk, z],
            z_ss.at[chunk, 0],
            z_rs.at[chunk, z],
            z_dev(z),
        )

    def core_copy(chunk):
        return remote(
            core_send.at[chunk],
            core_recv.at[chunk],
            core_ss.at[chunk],
            core_rs.at[chunk],
            core_dev,
        )

    def multiply(c):
        for half, d in steps:
            g_two_arrived(c, half, d).wait_recv()
        columns = jnp.concatenate(
            [g_all[c, half].reshape(NXY * TOK, HD) for half in (0, 1)], axis=1
        )

        def product(first):
            return jnp.dot(
                x_t[pl.ds(pl.multiple_of(first, 256), 256)], columns, preferred_element_type=F32
            )

        @pl.loop(0, 2)
        def _(i):
            core_send[c, rows(i * 256, 256)] = product((1 - core) * 512 + i * 256)

        core_copy(c).start()

        @pl.loop(0, 2)
        def _(i):
            half_own[c, rows(i * 256, 256)] = product(core * 512 + i * 256)

    def reduce_cores(c):
        core_copy(c).wait_recv()
        for j in range(NZ):
            z = (j % 2) * 4 + j // 2
            part = pl.ds(j * OWN, OWN)
            total = half_own[c, part] + core_recv[c, part]
            half_own[c, part] = total
            z_send[c, z] = total.astype(BF16)

        @pl.loop(1, NZ)
        def _(d):
            z_copy(c, z_peer(d), d).start()

    for half, d in steps:
        dkv_first(half, d).start()
    finish_queries(2)
    forward_chunk(1)
    take_input()
    multiply(0)
    sum_first()
    reduce_cores(0)
    finish_queries(3)
    forward_chunk(2)
    multiply(1)
    sum_second()
    reduce_cores(1)
    forward_chunk(3)
    multiply(2)
    forward_chunk(4)
    reduce_cores(2)
    multiply(3)
    reduce_cores(3)
    multiply(4)
    reduce_cores(4)

    for c in range(NCHUNK):
        def add_slot(d, total):
            z = z_peer(d)
            z_arrived(c, z).wait_recv()
            return total + z_recv[c, z].astype(F32)

        own_part = half_own[c, rows((z_lo * 2 + z_hi) * OWN, OWN)]
        grad_ref[:, c * CHUNK : (c + 1) * CHUNK] = lax.fori_loop(1, NZ, add_slot, own_part)

    for c in range(4):
        qo_copy(c).wait_send()
        st_copy(c).wait_send()
        dq_copy(c).wait_send()
    for half, d in steps:
        kv_one(half, d).wait_send()
        kv_two(half, d).wait_send()
        dkv_first(half, d).wait_send()
        dkv_second(half, d).wait_send()
        for c in range(NCHUNK):
            g_one(c, half, d).wait_send()
            g_two(c, half, d).wait_send()
        pltpu.make_async_copy(x_mid.at[0, 0], x_mid.at[0, 0], x1_ss.at[half, d]).wait()
        pltpu.make_async_copy(x_recv.at[0, 0, 0], x_recv.at[0, 0, 0], x0_ss.at[half, d]).wait()
        for e in (1, 2, 3):
            x_two(half, d, e).wait_send()

    for c in range(NCHUNK):
        core_copy(c).wait_send()

        @pl.loop(1, NZ)
        def _(d):
            z_copy(c, z_peer(d), d).wait_send()


def fused(order, x, q, k, v, o):
    vmem = pl.BlockSpec(memory_space=pltpu.VMEM)
    dma = pltpu.SemaphoreType.DMA
    scratch = [
        pltpu.VMEM((2, 4, 4, TOK, HD), BF16),
        pltpu.VMEM((HD, KEYS), BF16),
        pltpu.VMEM((2, 4, 4, 4, TOK, TOK), BF16),
        pltpu.VMEM((2, 4, 4, 4, TOK, TOK), BF16),
        pltpu.VMEM((ROWS, NXY * TOK), BF16),
        pltpu.VMEM((2, KEYS, 2 * SIDE), F32),
        pltpu.VMEM((2, KEYS, 2 * SIDE), F32),
        pltpu.VMEM((KEYS, 2 * HD), F32),
        pltpu.VMEM((2, 4, 4, TOK, HD), BF16),
        pltpu.VMEM((2, 4, 4, TOK, HD), BF16),
        pltpu.VMEM((2, 4, TOK, HD), F32),
        pltpu.VMEM((2, 4, TOK, HD), F32),
        pltpu.VMEM((4, 2, 2, SIDE, HD), BF16),
        pltpu.VMEM((4, 8, 2 * SIDE), F32),
        pltpu.VMEM((4, 8, 2 * SIDE), F32),
        pltpu.VMEM((4, HD, SIDE), F32),
        pltpu.VMEM((4, HD, SIDE), F32),
        pltpu.VMEM((4, HD, SIDE), F32),
        pltpu.VMEM((NCHUNK, 2, 4, 4, TOK, HD), BF16),
        pltpu.VMEM((NCHUNK, ROWS // 2, CHUNK), F32),
        pltpu.VMEM((NCHUNK, ROWS // 2, CHUNK), F32),
        pltpu.VMEM((NCHUNK, ROWS // 2, CHUNK), F32),
        pltpu.VMEM((NCHUNK, NZ, OWN, CHUNK), BF16),
        pltpu.VMEM((NCHUNK, NZ, OWN, CHUNK), BF16),
        dma((4,)),
        dma((4,)),
        dma((4,)),
        dma((4,)),
        dma((4,)),
        dma((4,)),
        dma((2, 4)),
        dma((2, 4)),
        dma((2, 4)),
        dma((2, 4)),
        dma((2, 4)),
        dma((2, 4)),
        dma((2, 4, 4)),
        dma((2, 4, 4)),
        dma((2, 4, 4)),
        dma((2, 4)),
        dma((NCHUNK, 2, 4)),
        dma((NCHUNK, 2, 4)),
        dma((NCHUNK, 2, 4)),
        dma((NCHUNK, 2, 4)),
        dma((2, 4)),
        dma((2, 4)),
        dma((2, 4)),
        dma((2, 4)),
        dma((NCHUNK,)),
        dma((NCHUNK,)),
        dma((NCHUNK, NZ)),
        dma((NCHUNK, NZ)),
    ]
    return pl.pallas_call(
        fused_kernel,
        name="attention_backward_and_weight_gradient",
        out_shape=jax.ShapeDtypeStruct((OWN, NCHUNK * CHUNK), F32),
        in_specs=[
            pl.BlockSpec(memory_space=pltpu.SMEM),
            pl.BlockSpec(memory_space=pl.ANY),
            vmem,
            vmem,
            vmem,
            vmem,
        ],
        out_specs=vmem,
        scratch_shapes=scratch,
        compiler_params=pltpu.CompilerParams(
            collective_id=0, has_side_effects=True, vmem_limit_bytes=60 * 2**20
        ),
    )(order, x, q, k, v, o)


def per_device(
    layer_input,
    query_rows,
    key_rows,
    value_rows,
    out_grad,
    block_order,
    master,
    moment_one,
    moment_two,
):
    grad_local = fused(
        block_order, layer_input[0], query_rows[0], key_rows[0], value_rows[0], out_grad[0]
    )
    new_one = BETA_ONE * moment_one + (1.0 - BETA_ONE) * grad_local
    new_two = BETA_TWO * moment_two + (1.0 - BETA_TWO) * grad_local * grad_local
    corr_one = 1.0 - BETA_ONE**STEP
    corr_two = 1.0 - BETA_TWO**STEP
    update = new_one / corr_one / (jnp.sqrt(new_two / corr_two) + EPSILON)
    new_master = master - LEARN_RATE * (update + DECAY * master)
    return (new_master, new_one, new_two)


def solution(mesh):
    rows = P("dp", "ctx", None)
    owned = P(("dp", "ctx"), None)
    return jax.shard_map(
        per_device,
        mesh=mesh,
        in_specs=(rows, rows, rows, rows, rows, P(), owned, owned, owned),
        out_specs=(owned, owned, owned),
        check_vma=False,
    )
```

```python
import functools
import math

import jax
import jax.numpy as jnp
from jax import lax
from jax.experimental import pallas as pl
from jax.experimental.pallas import tpu as pltpu
from jax.sharding import PartitionSpec as P

STEP = 10
NEG_FILL = -1e30
BETA_ONE = 0.9
BETA_TWO = 0.95
EPSILON = 1e-08
LEARN_RATE = 0.01
DECAY = 0.1

F32 = jnp.float32
BF16 = jnp.bfloat16
MESH = pl.DeviceIdType.MESH
ROW_CONTRACT = (((1,), (1,)), ((), ()))

TOK = 128
HD = 128
HALF = 64
NXY = 16
NCTX = 32
NZ = 8
CHUNK = 256
NCHUNK = 5
KEYS = NXY * TOK
KT = 256
SIDE = 256
LOG2E = math.log2(math.e)
OWN = 64
ROWS = 1024
SCALE = 1.0 / math.sqrt(HD)


def fused_kernel(
    order_ref,
    x_hbm,
    q_ref,
    k_ref,
    v_ref,
    o_ref,
    grad_ref,
    kv_all,
    k_t,
    x_mid,
    x_recv,
    x_t,
    s_scr,
    d_scr,
    dkv_acc,
    dkv_send,
    dkv_one,
    dkv_sum,
    dkv_two,
    qo_all,
    st_send,
    st_recv,
    dq_own,
    dq_send,
    dq_recv,
    g_all,
    core_send,
    core_recv,
    half_own,
    z_send,
    z_recv,
    qo_ss,
    qo_rs,
    st_ss,
    st_rs,
    dq_ss,
    dq_rs,
    kv1_ss,
    kv1_rs,
    kv2_ss,
    kv2_rs,
    x0_ss,
    x1_ss,
    x1_rs,
    x2_ss,
    x_rs,
    x_own_sem,
    g1_ss,
    g1_rs,
    g2_ss,
    g2_rs,
    dkv1_ss,
    dkv1_rs,
    dkv2_ss,
    dkv2_rs,
    core_ss,
    core_rs,
    z_ss,
    z_rs,
):
    dp = lax.axis_index("dp")
    ctx = lax.axis_index("ctx")
    core = lax.rem(dp, 2)
    z_lo = dp // 2
    z_hi = lax.rem(ctx, 2)
    plane = ctx // 2
    y = plane // 4
    x = lax.rem(plane, 4)
    z_me = z_hi * 4 + z_lo

    def plane_peer(d):
        return lax.rem(y + d // 4, 4) * 4 + lax.rem(x + lax.rem(d, 4), 4)

    def plane_dev(k):
        return (dp, k * 2 + z_hi)

    def z_peer(d):
        return lax.rem(z_me + d, NZ)

    def z_dev(z):
        return (lax.rem(z, 4) * 2 + core, plane * 2 + z // 4)

    zh_dev = (dp, plane * 2 + (1 - z_hi))
    place = (y, x)

    def line_dev(axis, i):
        return plane_dev(i * 4 + x if axis == 0 else y * 4 + i)

    def line_peer(axis, d):
        return lax.rem(place[axis] + d, 4)

    def remote(src, dst, ss, rs, target):
        return pltpu.make_async_remote_copy(
            src_ref=src,
            dst_ref=dst,
            send_sem=ss,
            recv_sem=rs,
            device_id=target,
            device_id_type=MESH,
        )

    def across(array, half, i):
        return array.at[half, :, i] if half == 0 else array.at[half, i]

    core_dev = (z_lo * 2 + (1 - core), ctx)

    barrier = pltpu.get_barrier_semaphore()

    @pl.loop(1, NXY)
    def _(d):
        pl.semaphore_signal(barrier, inc=1, device_id=plane_dev(plane_peer(d)), device_id_type=MESH)

    @pl.loop(1, NZ)
    def _(d):
        pl.semaphore_signal(barrier, inc=1, device_id=z_dev(z_peer(d)), device_id_type=MESH)

    pl.semaphore_signal(barrier, inc=1, device_id=core_dev, device_id_type=MESH)

    def rows(first, count):
        return pl.ds(pl.multiple_of(first, count), count)

    kv_all[0, y, x] = k_ref[...]
    kv_all[1, y, x] = v_ref[...]
    for c in range(4):
        for i in range(2):
            head = slice((2 * c + i) * HD, (2 * c + i + 1) * HD)
            qo_all[c, 0, 0, i * TOK : (i + 1) * TOK] = q_ref[:, head]
            qo_all[c, 1, 0, i * TOK : (i + 1) * TOK] = o_ref[:, head]

    pl.semaphore_wait(barrier, NXY - 1 + NZ - 1 + 1)

    def qo_copy(c):
        return remote(
            qo_all.at[c, :, 0], qo_all.at[c, :, 1], qo_ss.at[c], qo_rs.at[c], zh_dev
        )

    def st_copy(c):
        return remote(st_send.at[c], st_recv.at[c], st_ss.at[c], st_rs.at[c], zh_dev)

    def dq_copy(c):
        return remote(dq_send.at[c], dq_recv.at[c], dq_ss.at[c], dq_rs.at[c], zh_dev)

    def kv_one(half, d):
        piece = kv_all.at[half, y, x]
        return remote(
            piece,
            piece,
            kv1_ss.at[half, d],
            kv1_rs.at[half, place[half]],
            line_dev(half, line_peer(half, d)),
        )

    def kv_one_arrived(half, d):
        i = line_peer(half, d)
        piece = kv_all.at[half, i, x] if half == 0 else kv_all.at[half, y, i]
        return remote(piece, piece, kv1_ss.at[half, d], kv1_rs.at[half, i], line_dev(half, i))

    def kv_two(half, d):
        axis = 1 - half
        piece = across(kv_all, half, place[axis])
        return remote(
            piece,
            piece,
            kv2_ss.at[half, d],
            kv2_rs.at[half, place[axis]],
            line_dev(axis, line_peer(axis, d)),
        )

    def kv_two_arrived(half, d):
        axis = 1 - half
        i = line_peer(axis, d)
        piece = across(kv_all, half, i)
        return remote(piece, piece, kv2_ss.at[half, d], kv2_rs.at[half, i], line_dev(axis, i))

    def x_columns(half, low, row, col):
        first = (low * 2 + half) * (NCTX * OWN) + (row * 4 + col) * TOK
        return x_hbm.at[:, rows(first, TOK)]

    def x_start(half, d):
        i = line_peer(half, d)
        for e in range(4):
            j = lax.rem(place[1 - half] + e, 4)
            for low in range(4):
                target = x_recv.at[half, y, x, low] if e == 0 else x_mid.at[half, place[half], j, low]
                remote(
                    x_columns(half, low, i, j) if half == 0 else x_columns(half, low, j, i),
                    target,
                    x1_ss.at[half, d],
                    x_rs.at[half, y, x] if e == 0 else x1_rs.at[half, place[half], j],
                    line_dev(half, i),
                ).start()

    def x_start_line(half, d):
        axis = 1 - half
        i = line_peer(axis, d)
        for low in range(4):
            remote(
                x_columns(half, low, y, i) if half == 0 else x_columns(half, low, i, x),
                x_recv.at[half, y, x, low],
                x0_ss.at[half, d],
                x_rs.at[half, y, x],
                line_dev(axis, i),
            ).start()

    def x_own(half, low):
        return pltpu.make_async_copy(
            x_columns(half, low, y, x), x_recv.at[half, y, x, low], x_own_sem.at[half, low]
        )

    def x_two(half, d, e):
        axis = 1 - half
        i = line_peer(half, d)
        j = line_peer(axis, e)
        where = (i, x) if half == 0 else (y, i)
        return remote(
            x_mid.at[half, i, j],
            x_recv.at[half, where[0], where[1]],
            x2_ss.at[half, d, e],
            x_rs.at[half, where[0], where[1]],
            line_dev(axis, j),
        )

    def x_forward(half):
        for d in (1, 3, 2):
            i = line_peer(half, d)
            for e in (1, 3, 2):
                j = line_peer(1 - half, e)
                piece = x_mid.at[half, i, j]
                pltpu.make_async_copy(piece, piece, x1_rs.at[half, i, j]).wait()
                x_two(half, d, e).start()

    steps = [(half, d) for d in (1, 3, 2) for half in (0, 1)]
    for half, d in steps:
        kv_one(half, d).start()
    for c in range(4):
        qo_copy(c).start()
    for half in (0, 1):
        for d in (1, 3, 2):
            kv_one_arrived(half, d).wait_recv()
        for d in (1, 3, 2):
            kv_two(half, d).start()
    x_start(0, 1)
    x_start(1, 1)
    x_start(0, 3)
    x_start(1, 3)
    x_start(0, 2)
    x_start(1, 2)
    x_start_line(0, 1)
    x_start_line(1, 1)
    x_start_line(0, 3)
    x_start_line(1, 3)
    x_start_line(0, 2)
    x_start_line(1, 2)
    for half in (0, 1):
        for low in range(4):
            x_own(half, low).start()
    for half, d in steps:
        kv_two_arrived(half, d).wait_recv()

    lane = lax.broadcasted_iota(jnp.int32, (1, 2 * SIDE), 1)
    token = lax.rem(lane, TOK)
    other = plane * 2 + 1 - z_hi
    first_pos = jnp.where(lane < SIDE, order_ref[2 * ctx], order_ref[2 * other])
    second_pos = jnp.where(lane < SIDE, order_ref[2 * ctx + 1], order_ref[2 * other + 1])
    query_pos = jnp.where(token < HALF, first_pos, second_pos) * HALF + lax.rem(token, HALF)
    sub = lax.broadcasted_iota(jnp.int32, (HALF, 2 * SIDE), 0)

    @pl.loop(0, NXY)
    def _(b):
        k_t[:, rows(b * TOK, TOK)] = kv_all[0, b // 4, lax.rem(b, 4)].T

    def g_one(chunk, half, d):
        piece = g_all.at[chunk, half, y, x]
        return remote(
            piece,
            piece,
            g1_ss.at[chunk, half, d],
            g1_rs.at[chunk, half, place[half]],
            line_dev(half, line_peer(half, d)),
        )

    def g_one_arrived(chunk, half, d):
        i = line_peer(half, d)
        piece = g_all.at[chunk, half, i, x] if half == 0 else g_all.at[chunk, half, y, i]
        return remote(
            piece, piece, g1_ss.at[chunk, half, d], g1_rs.at[chunk, half, i], line_dev(half, i)
        )

    def g_two(chunk, half, d):
        axis = 1 - half
        piece = across(g_all.at[chunk], half, place[axis])
        return remote(
            piece,
            piece,
            g2_ss.at[chunk, half, d],
            g2_rs.at[chunk, half, place[axis]],
            line_dev(axis, line_peer(axis, d)),
        )

    def g_two_arrived(chunk, half, d):
        axis = 1 - half
        i = line_peer(axis, d)
        piece = across(g_all.at[chunk], half, i)
        return remote(
            piece, piece, g2_ss.at[chunk, half, d], g2_rs.at[chunk, half, i], line_dev(axis, i)
        )

    def send_chunk(chunk):
        for half, d in steps:
            g_one(chunk, half, d).start()

    def forward_chunk(chunk):
        for half in (0, 1):
            for d in (1, 3, 2):
                g_one_arrived(chunk, half, d).wait_recv()
            for d in (1, 3, 2):
                g_two(chunk, half, d).start()

    def dkv_first(half, d):
        i = line_peer(half, d)
        return remote(
            dkv_send.at[half, i] if half == 0 else dkv_send.at[half, :, i],
            dkv_one.at[half, place[half]],
            dkv1_ss.at[half, d],
            dkv1_rs.at[half, place[half]],
            line_dev(half, i),
        )

    def dkv_first_arrived(half, d):
        i = line_peer(half, d)
        return remote(
            dkv_one.at[half, i],
            dkv_one.at[half, i],
            dkv1_ss.at[half, d],
            dkv1_rs.at[half, i],
            line_dev(half, i),
        )

    def dkv_second(half, d):
        axis = 1 - half
        i = line_peer(axis, d)
        return remote(
            dkv_sum.at[half, i],
            dkv_two.at[half, place[axis]],
            dkv2_ss.at[half, d],
            dkv2_rs.at[half, place[axis]],
            line_dev(axis, i),
        )

    def dkv_second_arrived(half, d):
        axis = 1 - half
        i = line_peer(axis, d)
        return remote(
            dkv_two.at[half, i],
            dkv_two.at[half, i],
            dkv2_ss.at[half, d],
            dkv2_rs.at[half, i],
            line_dev(axis, i),
        )

    def key_tile(ref, half, t):
        return ref.at[half, t // 2, pl.ds(lax.rem(t, 2) * 2, 2)]

    def fold(a, op):
        return op(a.reshape(a.shape[0] // 8, 8, a.shape[1]), axis=0)

    def local_pass(c):
        slot = c % 2
        q_c = qo_all[c, 0].reshape(2 * SIDE, HD)
        o_c = qo_all[c, 1].reshape(2 * SIDE, HD)

        def scores_tile(t, top):
            first = pl.multiple_of(t * KT, KT)
            s = lax.dot_general(
                key_tile(kv_all, 0, t)[...].reshape(KT, HD),
                q_c,
                ROW_CONTRACT,
                preferred_element_type=F32,
            )
            d_scr[slot, pl.ds(first, KT)] = lax.dot_general(
                key_tile(kv_all, 1, t)[...].reshape(KT, HD),
                o_c,
                ROW_CONTRACT,
                preferred_element_type=F32,
            )
            for b in range(KT // HALF):
                owner = (t * 2 + b // 2) * 2 + z_hi
                limit = query_pos - order_ref[owner * 2 + b % 2] * HALF
                part = jnp.where(sub <= limit, s[b * HALF : (b + 1) * HALF], NEG_FILL)
                s_scr[slot, pl.ds(first + b * HALF, HALF)] = part
                top = jnp.maximum(top, fold(part, jnp.max))
            return top

        top = lax.fori_loop(0, KEYS // KT, scores_tile, jnp.full((8, 2 * SIDE), NEG_FILL, F32))
        top = jnp.max(top, axis=0, keepdims=True)

        def weights_tile(t, carried):
            total, inner = carried
            tile = pl.ds(pl.multiple_of(t * KT, KT), KT)
            e = jnp.exp2((s_scr[slot, tile] - top) * (SCALE * LOG2E))
            s_scr[slot, tile] = e
            return total + fold(e, jnp.sum), inner + fold(e * d_scr[slot, tile], jnp.sum)

        zero = jnp.zeros((8, 2 * SIDE), F32)
        total, inner = lax.fori_loop(0, KEYS // KT, weights_tile, (zero, zero))
        row = lax.broadcasted_iota(jnp.int32, (8, 2 * SIDE), 0)
        total = jnp.sum(total, axis=0, keepdims=True)
        inner = jnp.sum(inner, axis=0, keepdims=True)
        st_send[c] = jnp.where(row == 0, top, jnp.where(row == 1, total, inner))
        st_copy(c).start()

    def gradient_pass(c):
        slot = c % 2
        q_c = qo_all[c, 0].reshape(2 * SIDE, HD)
        o_c = qo_all[c, 1].reshape(2 * SIDE, HD)
        st_copy(c).wait_recv()

        mine_top, mine_total, mine_inner = (st_send[c, r : r + 1] for r in range(3))
        their_top, their_total, their_inner = (
            jnp.concatenate([st_recv[c, r : r + 1, SIDE:], st_recv[c, r : r + 1, :SIDE]], axis=1)
            for r in range(3)
        )
        top = jnp.maximum(mine_top, their_top)
        mine = jnp.exp2((mine_top - top) * (SCALE * LOG2E))
        theirs = jnp.exp2((their_top - top) * (SCALE * LOG2E))
        whole = 1.0 / (mine_total * mine + their_total * theirs)
        delta = (mine_inner * mine + their_inner * theirs) * whole
        inv = mine * whole

        def grads_tile(t, dq):
            tile = pl.ds(pl.multiple_of(t * KT, KT), KT)
            p = s_scr[slot, tile] * inv
            ds = (p * (d_scr[slot, tile] - delta) * SCALE).astype(BF16)
            dk = jnp.dot(ds, q_c, preferred_element_type=F32)
            dv = jnp.dot(p.astype(BF16), o_c, preferred_element_type=F32)
            if c == 0:
                dkv_acc[tile, :HD] = dk
                dkv_acc[tile, HD:] = dv
            elif c < 3:
                dkv_acc[tile, :HD] += dk
                dkv_acc[tile, HD:] += dv
            else:
                dk = (dkv_acc[tile, :HD] + dk).astype(BF16)
                dv = (dkv_acc[tile, HD:] + dv).astype(BF16)
                key_tile(dkv_send, 0, t)[...] = dk.reshape(2, TOK, HD)
                key_tile(dkv_send, 1, t)[...] = dv.reshape(2, TOK, HD)
            return dq + jnp.dot(k_t[:, tile], ds, preferred_element_type=F32)

        dq = lax.fori_loop(0, KEYS // KT, grads_tile, jnp.zeros((HD, 2 * SIDE), F32))
        dq_own[c] = dq[:, :SIDE]
        dq_send[c] = dq[:, SIDE:]
        dq_copy(c).start()

    def finish_queries(c):
        dq_copy(c).wait_recv()
        for i in range(2):
            part = slice(i * TOK, (i + 1) * TOK)
            g_all[c, i, y, x] = (dq_own[c, :, part] + dq_recv[c, :, part]).T.astype(BF16)
        send_chunk(c)

    for c in range(4):
        qo_copy(c).wait_recv()
        local_pass(c)
        if c > 0:
            gradient_pass(c - 1)
        if c == 1:
            x_forward(0)
            x_forward(1)
        if c > 1:
            finish_queries(c - 2)
        if c > 2:
            forward_chunk(c - 3)
    gradient_pass(3)
    def sum_first():
        for half in (0, 1):
            for d in (1, 3, 2):
                dkv_first_arrived(half, d).wait_recv()
            for j in range(4):
                piece = dkv_send[half, y, j] if half == 0 else dkv_send[half, j, x]
                total = piece.astype(F32)
                for d in (1, 3, 2):
                    total += dkv_one[half, line_peer(half, d), j].astype(F32)
                dkv_sum[half, j] = total
            for d in (1, 3, 2):
                dkv_second(half, d).start()

    def sum_second():
        for half in (0, 1):
            axis = 1 - half
            total = dkv_sum[half, place[axis]]
            for d in (1, 3, 2):
                dkv_second_arrived(half, d).wait_recv()
                total += dkv_two[half, line_peer(axis, d)]
            g_all[4, half, y, x] = total.astype(BF16)
        send_chunk(4)

    def transpose_slot(row, col):
        for half in (0, 1):
            for low in range(4):
                first = (half * 4 + low) * TOK
                x_t[first : first + TOK, rows((row * 4 + col) * TOK, TOK)] = x_recv[
                    half, row, col, low
                ].T

    def take_input():
        for half in (0, 1):
            for low in range(4):
                x_own(half, low).wait()
        transpose_slot(y, x)

        @pl.loop(1, NXY)
        def _(d):
            k = plane_peer(d)
            row, col = k // 4, lax.rem(k, 4)
            for half in (0, 1):
                piece = x_recv.at[half, row, col]
                pltpu.make_async_copy(piece, piece, x_rs.at[half, row, col]).wait()
            transpose_slot(row, col)

    def z_copy(chunk, z, d):
        return remote(
            z_send.at[chunk, z],
            z_recv.at[chunk, z_me],
            z_ss.at[chunk, d],
            z_rs.at[chunk, z_me],
            z_dev(z),
        )

    def z_arrived(chunk, z):
        return remote(
            z_send.at[chunk, z],
            z_recv.at[chunk, z],
            z_ss.at[chunk, 0],
            z_rs.at[chunk, z],
            z_dev(z),
        )

    def core_copy(chunk):
        return remote(
            core_send.at[chunk],
            core_recv.at[chunk],
            core_ss.at[chunk],
            core_rs.at[chunk],
            core_dev,
        )

    def multiply(c):
        for half, d in steps:
            g_two_arrived(c, half, d).wait_recv()
        columns = jnp.concatenate(
            [g_all[c, half].reshape(NXY * TOK, HD) for half in (0, 1)], axis=1
        )

        def product(first):
            return jnp.dot(
                x_t[pl.ds(pl.multiple_of(first, 256), 256)], columns, preferred_element_type=F32
            )

        @pl.loop(0, 2)
        def _(i):
            core_send[c, rows(i * 256, 256)] = product((1 - core) * 512 + i * 256)

        core_copy(c).start()

        @pl.loop(0, 2)
        def _(i):
            half_own[c, rows(i * 256, 256)] = product(core * 512 + i * 256)

    def reduce_cores(c):
        core_copy(c).wait_recv()
        for j in range(NZ):
            z = (j % 2) * 4 + j // 2
            part = pl.ds(j * OWN, OWN)
            total = half_own[c, part] + core_recv[c, part]
            half_own[c, part] = total
            z_send[c, z] = total.astype(BF16)

        @pl.loop(1, NZ)
        def _(d):
            z_copy(c, z_peer(d), d).start()

    for half, d in steps:
        dkv_first(half, d).start()
    finish_queries(2)
    forward_chunk(1)
    sum_first()
    take_input()
    multiply(0)
    reduce_cores(0)
    finish_queries(3)
    forward_chunk(2)
    multiply(1)
    sum_second()
    forward_chunk(3)
    reduce_cores(1)
    multiply(2)
    forward_chunk(4)
    reduce_cores(2)
    multiply(3)
    reduce_cores(3)
    multiply(4)
    reduce_cores(4)

    for c in range(4):
        qo_copy(c).wait_send()
        st_copy(c).wait_send()
        dq_copy(c).wait_send()
    for half, d in steps:
        kv_one(half, d).wait_send()
        kv_two(half, d).wait_send()
        dkv_first(half, d).wait_send()
        dkv_second(half, d).wait_send()
        for c in range(NCHUNK):
            g_one(c, half, d).wait_send()
            g_two(c, half, d).wait_send()
        pltpu.make_async_copy(x_mid.at[0, 0], x_mid.at[0, 0], x1_ss.at[half, d]).wait()
        pltpu.make_async_copy(x_recv.at[0, 0, 0], x_recv.at[0, 0, 0], x0_ss.at[half, d]).wait()
        for e in (1, 2, 3):
            x_two(half, d, e).wait_send()

    for c in range(NCHUNK):
        core_copy(c).wait_send()

    for c in range(NCHUNK):
        def add_slot(d, total):
            z = z_peer(d)
            z_arrived(c, z).wait_recv()
            return total + z_recv[c, z].astype(F32)

        own_part = half_own[c, rows((z_lo * 2 + z_hi) * OWN, OWN)]
        grad_ref[:, c * CHUNK : (c + 1) * CHUNK] = lax.fori_loop(1, NZ, add_slot, own_part)

    for c in range(NCHUNK):
        @pl.loop(1, NZ)
        def _(d):
            z_copy(c, z_peer(d), d).wait_send()


def fused(order, x, q, k, v, o):
    vmem = pl.BlockSpec(memory_space=pltpu.VMEM)
    dma = pltpu.SemaphoreType.DMA
    scratch = [
        pltpu.VMEM((2, 4, 4, TOK, HD), BF16),
        pltpu.VMEM((HD, KEYS), BF16),
        pltpu.VMEM((2, 4, 4, 4, TOK, TOK), BF16),
        pltpu.VMEM((2, 4, 4, 4, TOK, TOK), BF16),
        pltpu.VMEM((ROWS, NXY * TOK), BF16),
        pltpu.VMEM((2, KEYS, 2 * SIDE), F32),
        pltpu.VMEM((2, KEYS, 2 * SIDE), F32),
        pltpu.VMEM((KEYS, 2 * HD), F32),
        pltpu.VMEM((2, 4, 4, TOK, HD), BF16),
        pltpu.VMEM((2, 4, 4, TOK, HD), BF16),
        pltpu.VMEM((2, 4, TOK, HD), F32),
        pltpu.VMEM((2, 4, TOK, HD), F32),
        pltpu.VMEM((4, 2, 2, SIDE, HD), BF16),
        pltpu.VMEM((4, 8, 2 * SIDE), F32),
        pltpu.VMEM((4, 8, 2 * SIDE), F32),
        pltpu.VMEM((4, HD, SIDE), F32),
        pltpu.VMEM((4, HD, SIDE), F32),
        pltpu.VMEM((4, HD, SIDE), F32),
        pltpu.VMEM((NCHUNK, 2, 4, 4, TOK, HD), BF16),
        pltpu.VMEM((NCHUNK, ROWS // 2, CHUNK), F32),
        pltpu.VMEM((NCHUNK, ROWS // 2, CHUNK), F32),
        pltpu.VMEM((NCHUNK, ROWS // 2, CHUNK), F32),
        pltpu.VMEM((NCHUNK, NZ, OWN, CHUNK), BF16),
        pltpu.VMEM((NCHUNK, NZ, OWN, CHUNK), BF16),
        dma((4,)),
        dma((4,)),
        dma((4,)),
        dma((4,)),
        dma((4,)),
        dma((4,)),
        dma((2, 4)),
        dma((2, 4)),
        dma((2, 4)),
        dma((2, 4)),
        dma((2, 4)),
        dma((2, 4)),
        dma((2, 4, 4)),
        dma((2, 4, 4)),
        dma((2, 4, 4)),
        dma((2, 4)),
        dma((NCHUNK, 2, 4)),
        dma((NCHUNK, 2, 4)),
        dma((NCHUNK, 2, 4)),
        dma((NCHUNK, 2, 4)),
        dma((2, 4)),
        dma((2, 4)),
        dma((2, 4)),
        dma((2, 4)),
        dma((NCHUNK,)),
        dma((NCHUNK,)),
        dma((NCHUNK, NZ)),
        dma((NCHUNK, NZ)),
    ]
    return pl.pallas_call(
        fused_kernel,
        name="attention_backward_and_weight_gradient",
        out_shape=jax.ShapeDtypeStruct((OWN, NCHUNK * CHUNK), F32),
        in_specs=[
            pl.BlockSpec(memory_space=pltpu.SMEM),
            pl.BlockSpec(memory_space=pl.ANY),
            vmem,
            vmem,
            vmem,
            vmem,
        ],
        out_specs=vmem,
        scratch_shapes=scratch,
        compiler_params=pltpu.CompilerParams(
            collective_id=0, has_side_effects=True, vmem_limit_bytes=60 * 2**20
        ),
    )(order, x, q, k, v, o)


def per_device(
    layer_input,
    query_rows,
    key_rows,
    value_rows,
    out_grad,
    block_order,
    master,
    moment_one,
    moment_two,
):
    grad_local = fused(
        block_order, layer_input[0], query_rows[0], key_rows[0], value_rows[0], out_grad[0]
    )
    new_one = BETA_ONE * moment_one + (1.0 - BETA_ONE) * grad_local
    new_two = BETA_TWO * moment_two + (1.0 - BETA_TWO) * grad_local * grad_local
    corr_one = 1.0 - BETA_ONE**STEP
    corr_two = 1.0 - BETA_TWO**STEP
    update = new_one / corr_one / (jnp.sqrt(new_two / corr_two) + EPSILON)
    new_master = master - LEARN_RATE * (update + DECAY * master)
    return (new_master, new_one, new_two)


def solution(mesh):
    rows = P("dp", "ctx", None)
    owned = P(("dp", "ctx"), None)
    return jax.shard_map(
        per_device,
        mesh=mesh,
        in_specs=(rows, rows, rows, rows, rows, P(), owned, owned, owned),
        out_specs=(owned, owned, owned),
        check_vma=False,
    )
```

```python
import functools
import math

import jax
import jax.numpy as jnp
from jax import lax
from jax.experimental import pallas as pl
from jax.experimental.pallas import tpu as pltpu
from jax.sharding import PartitionSpec as P

STEP = 10
NEG_FILL = -1e30
BETA_ONE = 0.9
BETA_TWO = 0.95
EPSILON = 1e-08
LEARN_RATE = 0.01
DECAY = 0.1

F32 = jnp.float32
BF16 = jnp.bfloat16
MESH = pl.DeviceIdType.MESH
ROW_CONTRACT = (((1,), (1,)), ((), ()))

TOK = 128
HD = 128
HALF = 64
NXY = 16
NCTX = 32
NZ = 8
CHUNK = 256
NCHUNK = 5
KEYS = NXY * TOK
KT = 256
SIDE = 256
LOG2E = math.log2(math.e)
OWN = 64
ROWS = 1024
SCALE = 1.0 / math.sqrt(HD)


def fused_kernel(
    order_ref,
    x_hbm,
    q_ref,
    k_ref,
    v_ref,
    o_ref,
    grad_ref,
    kv_all,
    k_t,
    x_mid,
    x_recv,
    x_t,
    s_scr,
    d_scr,
    dkv_acc,
    dkv_send,
    dkv_one,
    dkv_sum,
    dkv_two,
    qo_all,
    st_send,
    st_recv,
    dq_own,
    dq_send,
    dq_recv,
    g_all,
    core_send,
    core_recv,
    half_own,
    z_send,
    z_recv,
    qo_ss,
    qo_rs,
    st_ss,
    st_rs,
    dq_ss,
    dq_rs,
    kv1_ss,
    kv1_rs,
    kv2_ss,
    kv2_rs,
    x0_ss,
    x1_ss,
    x1_rs,
    x2_ss,
    x_rs,
    x_own_sem,
    g1_ss,
    g1_rs,
    g2_ss,
    g2_rs,
    dkv1_ss,
    dkv1_rs,
    dkv2_ss,
    dkv2_rs,
    core_ss,
    core_rs,
    z_ss,
    z_rs,
):
    dp = lax.axis_index("dp")
    ctx = lax.axis_index("ctx")
    core = lax.rem(dp, 2)
    z_lo = dp // 2
    z_hi = lax.rem(ctx, 2)
    plane = ctx // 2
    y = plane // 4
    x = lax.rem(plane, 4)
    z_me = z_hi * 4 + z_lo

    def plane_peer(d):
        return lax.rem(y + d // 4, 4) * 4 + lax.rem(x + lax.rem(d, 4), 4)

    def plane_dev(k):
        return (dp, k * 2 + z_hi)

    def z_peer(d):
        return lax.rem(z_me + d, NZ)

    def z_dev(z):
        return (lax.rem(z, 4) * 2 + core, plane * 2 + z // 4)

    zh_dev = (dp, plane * 2 + (1 - z_hi))
    place = (y, x)

    def line_dev(axis, i):
        return plane_dev(i * 4 + x if axis == 0 else y * 4 + i)

    def line_peer(axis, d):
        return lax.rem(place[axis] + d, 4)

    def remote(src, dst, ss, rs, target):
        return pltpu.make_async_remote_copy(
            src_ref=src,
            dst_ref=dst,
            send_sem=ss,
            recv_sem=rs,
            device_id=target,
            device_id_type=MESH,
        )

    def across(array, half, i):
        return array.at[half, :, i] if half == 0 else array.at[half, i]

    core_dev = (z_lo * 2 + (1 - core), ctx)

    barrier = pltpu.get_barrier_semaphore()

    @pl.loop(1, NXY)
    def _(d):
        pl.semaphore_signal(barrier, inc=1, device_id=plane_dev(plane_peer(d)), device_id_type=MESH)

    @pl.loop(1, NZ)
    def _(d):
        pl.semaphore_signal(barrier, inc=1, device_id=z_dev(z_peer(d)), device_id_type=MESH)

    pl.semaphore_signal(barrier, inc=1, device_id=core_dev, device_id_type=MESH)

    def rows(first, count):
        return pl.ds(pl.multiple_of(first, count), count)

    kv_all[0, y, x] = k_ref[...]
    kv_all[1, y, x] = v_ref[...]
    for c in range(4):
        for i in range(2):
            head = slice((2 * c + i) * HD, (2 * c + i + 1) * HD)
            qo_all[c, 0, 0, i * TOK : (i + 1) * TOK] = q_ref[:, head]
            qo_all[c, 1, 0, i * TOK : (i + 1) * TOK] = o_ref[:, head]

    pl.semaphore_wait(barrier, NXY - 1 + NZ - 1 + 1)

    def qo_copy(c):
        return remote(
            qo_all.at[c, :, 0], qo_all.at[c, :, 1], qo_ss.at[c], qo_rs.at[c], zh_dev
        )

    def st_copy(c):
        return remote(st_send.at[c], st_recv.at[c], st_ss.at[c], st_rs.at[c], zh_dev)

    def dq_copy(c):
        return remote(dq_send.at[c], dq_recv.at[c], dq_ss.at[c], dq_rs.at[c], zh_dev)

    def kv_one(half, d):
        piece = kv_all.at[half, y, x]
        return remote(
            piece,
            piece,
            kv1_ss.at[half, d],
            kv1_rs.at[half, place[half]],
            line_dev(half, line_peer(half, d)),
        )

    def kv_one_arrived(half, d):
        i = line_peer(half, d)
        piece = kv_all.at[half, i, x] if half == 0 else kv_all.at[half, y, i]
        return remote(piece, piece, kv1_ss.at[half, d], kv1_rs.at[half, i], line_dev(half, i))

    def kv_two(half, d):
        axis = 1 - half
        piece = across(kv_all, half, place[axis])
        return remote(
            piece,
            piece,
            kv2_ss.at[half, d],
            kv2_rs.at[half, place[axis]],
            line_dev(axis, line_peer(axis, d)),
        )

    def kv_two_arrived(half, d):
        axis = 1 - half
        i = line_peer(axis, d)
        piece = across(kv_all, half, i)
        return remote(piece, piece, kv2_ss.at[half, d], kv2_rs.at[half, i], line_dev(axis, i))

    def x_columns(half, low, row, col):
        first = (low * 2 + half) * (NCTX * OWN) + (row * 4 + col) * TOK
        return x_hbm.at[:, rows(first, TOK)]

    def x_start(half, d):
        i = line_peer(half, d)
        for e in range(4):
            j = lax.rem(place[1 - half] + e, 4)
            for low in range(4):
                target = x_recv.at[half, y, x, low] if e == 0 else x_mid.at[half, place[half], j, low]
                remote(
                    x_columns(half, low, i, j) if half == 0 else x_columns(half, low, j, i),
                    target,
                    x1_ss.at[half, d],
                    x_rs.at[half, y, x] if e == 0 else x1_rs.at[half, place[half], j],
                    line_dev(half, i),
                ).start()

    def x_start_line(half, d):
        axis = 1 - half
        i = line_peer(axis, d)
        for low in range(4):
            remote(
                x_columns(half, low, y, i) if half == 0 else x_columns(half, low, i, x),
                x_recv.at[half, y, x, low],
                x0_ss.at[half, d],
                x_rs.at[half, y, x],
                line_dev(axis, i),
            ).start()

    def x_own(half, low):
        return pltpu.make_async_copy(
            x_columns(half, low, y, x), x_recv.at[half, y, x, low], x_own_sem.at[half, low]
        )

    def x_two(half, d, e):
        axis = 1 - half
        i = line_peer(half, d)
        j = line_peer(axis, e)
        where = (i, x) if half == 0 else (y, i)
        return remote(
            x_mid.at[half, i, j],
            x_recv.at[half, where[0], where[1]],
            x2_ss.at[half, d, e],
            x_rs.at[half, where[0], where[1]],
            line_dev(axis, j),
        )

    def x_forward(half):
        for d in (1, 3, 2):
            i = line_peer(half, d)
            for e in (1, 3, 2):
                j = line_peer(1 - half, e)
                piece = x_mid.at[half, i, j]
                pltpu.make_async_copy(piece, piece, x1_rs.at[half, i, j]).wait()
                x_two(half, d, e).start()

    steps = [(half, d) for d in (1, 3, 2) for half in (0, 1)]
    for half, d in steps:
        kv_one(half, d).start()
    for c in range(4):
        qo_copy(c).start()
    for half in (0, 1):
        for d in (1, 3, 2):
            kv_one_arrived(half, d).wait_recv()
        for d in (1, 3, 2):
            kv_two(half, d).start()
    x_start(0, 1)
    x_start(1, 1)
    x_start(0, 3)
    x_start(1, 3)
    x_start(0, 2)
    x_start(1, 2)
    x_start_line(0, 1)
    x_start_line(1, 1)
    x_start_line(0, 3)
    x_start_line(1, 3)
    x_start_line(0, 2)
    x_start_line(1, 2)
    for half in (0, 1):
        for low in range(4):
            x_own(half, low).start()
    for half, d in steps:
        kv_two_arrived(half, d).wait_recv()

    lane = lax.broadcasted_iota(jnp.int32, (1, 2 * SIDE), 1)
    token = lax.rem(lane, TOK)
    other = plane * 2 + 1 - z_hi
    first_pos = jnp.where(lane < SIDE, order_ref[2 * ctx], order_ref[2 * other])
    second_pos = jnp.where(lane < SIDE, order_ref[2 * ctx + 1], order_ref[2 * other + 1])
    query_pos = jnp.where(token < HALF, first_pos, second_pos) * HALF + lax.rem(token, HALF)
    sub = lax.broadcasted_iota(jnp.int32, (HALF, 2 * SIDE), 0)

    @pl.loop(0, NXY)
    def _(b):
        k_t[:, rows(b * TOK, TOK)] = kv_all[0, b // 4, lax.rem(b, 4)].T

    def g_one(chunk, half, d):
        piece = g_all.at[chunk, half, y, x]
        return remote(
            piece,
            piece,
            g1_ss.at[chunk, half, d],
            g1_rs.at[chunk, half, place[half]],
            line_dev(half, line_peer(half, d)),
        )

    def g_one_arrived(chunk, half, d):
        i = line_peer(half, d)
        piece = g_all.at[chunk, half, i, x] if half == 0 else g_all.at[chunk, half, y, i]
        return remote(
            piece, piece, g1_ss.at[chunk, half, d], g1_rs.at[chunk, half, i], line_dev(half, i)
        )

    def g_two(chunk, half, d):
        axis = 1 - half
        piece = across(g_all.at[chunk], half, place[axis])
        return remote(
            piece,
            piece,
            g2_ss.at[chunk, half, d],
            g2_rs.at[chunk, half, place[axis]],
            line_dev(axis, line_peer(axis, d)),
        )

    def g_two_arrived(chunk, half, d):
        axis = 1 - half
        i = line_peer(axis, d)
        piece = across(g_all.at[chunk], half, i)
        return remote(
            piece, piece, g2_ss.at[chunk, half, d], g2_rs.at[chunk, half, i], line_dev(axis, i)
        )

    def send_chunk(chunk):
        for half, d in steps:
            g_one(chunk, half, d).start()

    def forward_chunk(chunk):
        for half in (0, 1):
            for d in (1, 3, 2):
                g_one_arrived(chunk, half, d).wait_recv()
            for d in (1, 3, 2):
                g_two(chunk, half, d).start()

    def dkv_first(half, d):
        i = line_peer(half, d)
        return remote(
            dkv_send.at[half, i] if half == 0 else dkv_send.at[half, :, i],
            dkv_one.at[half, place[half]],
            dkv1_ss.at[half, d],
            dkv1_rs.at[half, place[half]],
            line_dev(half, i),
        )

    def dkv_first_arrived(half, d):
        i = line_peer(half, d)
        return remote(
            dkv_one.at[half, i],
            dkv_one.at[half, i],
            dkv1_ss.at[half, d],
            dkv1_rs.at[half, i],
            line_dev(half, i),
        )

    def dkv_second(half, d):
        axis = 1 - half
        i = line_peer(axis, d)
        return remote(
            dkv_sum.at[half, i],
            dkv_two.at[half, place[axis]],
            dkv2_ss.at[half, d],
            dkv2_rs.at[half, place[axis]],
            line_dev(axis, i),
        )

    def dkv_second_arrived(half, d):
        axis = 1 - half
        i = line_peer(axis, d)
        return remote(
            dkv_two.at[half, i],
            dkv_two.at[half, i],
            dkv2_ss.at[half, d],
            dkv2_rs.at[half, i],
            line_dev(axis, i),
        )

    def key_tile(ref, half, t):
        return ref.at[half, t // 2, pl.ds(lax.rem(t, 2) * 2, 2)]

    def fold(a, op):
        return op(a.reshape(a.shape[0] // 8, 8, a.shape[1]), axis=0)

    def local_pass(c):
        slot = c % 2
        q_c = qo_all[c, 0].reshape(2 * SIDE, HD)
        o_c = qo_all[c, 1].reshape(2 * SIDE, HD)

        def scores_tile(t, top):
            first = pl.multiple_of(t * KT, KT)
            s = lax.dot_general(
                key_tile(kv_all, 0, t)[...].reshape(KT, HD),
                q_c,
                ROW_CONTRACT,
                preferred_element_type=F32,
            )
            d_scr[slot, pl.ds(first, KT)] = lax.dot_general(
                key_tile(kv_all, 1, t)[...].reshape(KT, HD),
                o_c,
                ROW_CONTRACT,
                preferred_element_type=F32,
            )
            for b in range(KT // HALF):
                owner = (t * 2 + b // 2) * 2 + z_hi
                limit = query_pos - order_ref[owner * 2 + b % 2] * HALF
                part = jnp.where(sub <= limit, s[b * HALF : (b + 1) * HALF], NEG_FILL)
                s_scr[slot, pl.ds(first + b * HALF, HALF)] = part
                top = jnp.maximum(top, fold(part, jnp.max))
            return top

        top = lax.fori_loop(0, KEYS // KT, scores_tile, jnp.full((8, 2 * SIDE), NEG_FILL, F32))
        top = jnp.max(top, axis=0, keepdims=True)

        def weights_tile(t, carried):
            total, inner = carried
            tile = pl.ds(pl.multiple_of(t * KT, KT), KT)
            e = jnp.exp2((s_scr[slot, tile] - top) * (SCALE * LOG2E))
            s_scr[slot, tile] = e
            return total + fold(e, jnp.sum), inner + fold(e * d_scr[slot, tile], jnp.sum)

        zero = jnp.zeros((8, 2 * SIDE), F32)
        total, inner = lax.fori_loop(0, KEYS // KT, weights_tile, (zero, zero))
        row = lax.broadcasted_iota(jnp.int32, (8, 2 * SIDE), 0)
        total = jnp.sum(total, axis=0, keepdims=True)
        inner = jnp.sum(inner, axis=0, keepdims=True)
        st_send[c] = jnp.where(row == 0, top, jnp.where(row == 1, total, inner))
        st_copy(c).start()

    def gradient_pass(c):
        slot = c % 2
        q_c = qo_all[c, 0].reshape(2 * SIDE, HD)
        o_c = qo_all[c, 1].reshape(2 * SIDE, HD)
        st_copy(c).wait_recv()

        mine_top, mine_total, mine_inner = (st_send[c, r : r + 1] for r in range(3))
        their_top, their_total, their_inner = (
            jnp.concatenate([st_recv[c, r : r + 1, SIDE:], st_recv[c, r : r + 1, :SIDE]], axis=1)
            for r in range(3)
        )
        top = jnp.maximum(mine_top, their_top)
        mine = jnp.exp2((mine_top - top) * (SCALE * LOG2E))
        theirs = jnp.exp2((their_top - top) * (SCALE * LOG2E))
        whole = 1.0 / (mine_total * mine + their_total * theirs)
        delta = (mine_inner * mine + their_inner * theirs) * whole
        inv = mine * whole

        def grads_tile(t, dq):
            tile = pl.ds(pl.multiple_of(t * KT, KT), KT)
            p = s_scr[slot, tile] * inv
            ds = (p * (d_scr[slot, tile] - delta) * SCALE).astype(BF16)
            dk = jnp.dot(ds, q_c, preferred_element_type=F32)
            dv = jnp.dot(p.astype(BF16), o_c, preferred_element_type=F32)
            if c == 0:
                dkv_acc[tile, :HD] = dk
                dkv_acc[tile, HD:] = dv
            elif c < 3:
                dkv_acc[tile, :HD] += dk
                dkv_acc[tile, HD:] += dv
            else:
                dk = (dkv_acc[tile, :HD] + dk).astype(BF16)
                dv = (dkv_acc[tile, HD:] + dv).astype(BF16)
                key_tile(dkv_send, 0, t)[...] = dk.reshape(2, TOK, HD)
                key_tile(dkv_send, 1, t)[...] = dv.reshape(2, TOK, HD)
            return dq + jnp.dot(k_t[:, tile], ds, preferred_element_type=F32)

        dq = lax.fori_loop(0, KEYS // KT, grads_tile, jnp.zeros((HD, 2 * SIDE), F32))
        dq_own[c] = dq[:, :SIDE]
        dq_send[c] = dq[:, SIDE:]
        dq_copy(c).start()

    def finish_queries(c):
        dq_copy(c).wait_recv()
        for i in range(2):
            part = slice(i * TOK, (i + 1) * TOK)
            g_all[c, i, y, x] = (dq_own[c, :, part] + dq_recv[c, :, part]).T.astype(BF16)
        send_chunk(c)

    for c in range(4):
        qo_copy(c).wait_recv()
        local_pass(c)
        if c > 0:
            gradient_pass(c - 1)
        if c == 1:
            x_forward(0)
            x_forward(1)
        if c > 1:
            finish_queries(c - 2)
        if c > 2:
            forward_chunk(c - 3)
    gradient_pass(3)
    def sum_first():
        for half in (0, 1):
            for d in (1, 3, 2):
                dkv_first_arrived(half, d).wait_recv()
            for j in range(4):
                piece = dkv_send[half, y, j] if half == 0 else dkv_send[half, j, x]
                total = piece.astype(F32)
                for d in (1, 3, 2):
                    total += dkv_one[half, line_peer(half, d), j].astype(F32)
                dkv_sum[half, j] = total
            for d in (1, 3, 2):
                dkv_second(half, d).start()

    def sum_second():
        for half in (0, 1):
            axis = 1 - half
            total = dkv_sum[half, place[axis]]
            for d in (1, 3, 2):
                dkv_second_arrived(half, d).wait_recv()
                total += dkv_two[half, line_peer(axis, d)]
            g_all[4, half, y, x] = total.astype(BF16)
        send_chunk(4)

    def transpose_slot(row, col):
        for half in (0, 1):
            for low in range(4):
                first = (half * 4 + low) * TOK
                x_t[first : first + TOK, rows((row * 4 + col) * TOK, TOK)] = x_recv[
                    half, row, col, low
                ].T

    def take_input():
        for half in (0, 1):
            for low in range(4):
                x_own(half, low).wait()
        transpose_slot(y, x)

        @pl.loop(1, NXY)
        def _(d):
            k = plane_peer(d)
            row, col = k // 4, lax.rem(k, 4)
            for half in (0, 1):
                piece = x_recv.at[half, row, col]
                pltpu.make_async_copy(piece, piece, x_rs.at[half, row, col]).wait()
            transpose_slot(row, col)

    def z_copy(chunk, z, d):
        return remote(
            z_send.at[chunk, z],
            z_recv.at[chunk, z_me],
            z_ss.at[chunk, d],
            z_rs.at[chunk, z_me],
            z_dev(z),
        )

    def z_arrived(chunk, z):
        return remote(
            z_send.at[chunk, z],
            z_recv.at[chunk, z],
            z_ss.at[chunk, 0],
            z_rs.at[chunk, z],
            z_dev(z),
        )

    def core_copy(chunk):
        return remote(
            core_send.at[chunk],
            core_recv.at[chunk],
            core_ss.at[chunk],
            core_rs.at[chunk],
            core_dev,
        )

    def multiply(c):
        for half, d in steps:
            g_two_arrived(c, half, d).wait_recv()
        columns = jnp.concatenate(
            [g_all[c, half].reshape(NXY * TOK, HD) for half in (0, 1)], axis=1
        )

        def product(first):
            return jnp.dot(
                x_t[pl.ds(pl.multiple_of(first, 256), 256)], columns, preferred_element_type=F32
            )

        @pl.loop(0, 2)
        def _(i):
            core_send[c, rows(i * 256, 256)] = product((1 - core) * 512 + i * 256)

        core_copy(c).start()

        @pl.loop(0, 2)
        def _(i):
            half_own[c, rows(i * 256, 256)] = product(core * 512 + i * 256)

    def reduce_cores(c):
        core_copy(c).wait_recv()
        for j in range(NZ):
            z = (j % 2) * 4 + j // 2
            part = pl.ds(j * OWN, OWN)
            total = half_own[c, part] + core_recv[c, part]
            half_own[c, part] = total
            z_send[c, z] = total.astype(BF16)

        @pl.loop(1, NZ)
        def _(d):
            z_copy(c, z_peer(d), d).start()

    for half, d in steps:
        dkv_first(half, d).start()
    finish_queries(2)
    forward_chunk(1)
    sum_first()
    finish_queries(3)
    take_input()
    multiply(0)
    reduce_cores(0)
    forward_chunk(2)
    multiply(1)
    sum_second()
    forward_chunk(3)
    reduce_cores(1)
    multiply(2)
    forward_chunk(4)
    reduce_cores(2)
    multiply(3)
    reduce_cores(3)
    multiply(4)
    reduce_cores(4)

    for c in range(4):
        qo_copy(c).wait_send()
        st_copy(c).wait_send()
        dq_copy(c).wait_send()
    for half, d in steps:
        kv_one(half, d).wait_send()
        kv_two(half, d).wait_send()
        dkv_first(half, d).wait_send()
        dkv_second(half, d).wait_send()
        for c in range(NCHUNK):
            g_one(c, half, d).wait_send()
            g_two(c, half, d).wait_send()
        pltpu.make_async_copy(x_mid.at[0, 0], x_mid.at[0, 0], x1_ss.at[half, d]).wait()
        pltpu.make_async_copy(x_recv.at[0, 0, 0], x_recv.at[0, 0, 0], x0_ss.at[half, d]).wait()
        for e in (1, 2, 3):
            x_two(half, d, e).wait_send()

    for c in range(NCHUNK):
        core_copy(c).wait_send()

    for c in range(NCHUNK):
        def add_slot(d, total):
            z = z_peer(d)
            z_arrived(c, z).wait_recv()
            return total + z_recv[c, z].astype(F32)

        own_part = half_own[c, rows((z_lo * 2 + z_hi) * OWN, OWN)]
        grad_ref[:, c * CHUNK : (c + 1) * CHUNK] = lax.fori_loop(1, NZ, add_slot, own_part)

    for c in range(NCHUNK):
        @pl.loop(1, NZ)
        def _(d):
            z_copy(c, z_peer(d), d).wait_send()


def fused(order, x, q, k, v, o):
    vmem = pl.BlockSpec(memory_space=pltpu.VMEM)
    dma = pltpu.SemaphoreType.DMA
    scratch = [
        pltpu.VMEM((2, 4, 4, TOK, HD), BF16),
        pltpu.VMEM((HD, KEYS), BF16),
        pltpu.VMEM((2, 4, 4, 4, TOK, TOK), BF16),
        pltpu.VMEM((2, 4, 4, 4, TOK, TOK), BF16),
        pltpu.VMEM((ROWS, NXY * TOK), BF16),
        pltpu.VMEM((2, KEYS, 2 * SIDE), F32),
        pltpu.VMEM((2, KEYS, 2 * SIDE), F32),
        pltpu.VMEM((KEYS, 2 * HD), F32),
        pltpu.VMEM((2, 4, 4, TOK, HD), BF16),
        pltpu.VMEM((2, 4, 4, TOK, HD), BF16),
        pltpu.VMEM((2, 4, TOK, HD), F32),
        pltpu.VMEM((2, 4, TOK, HD), F32),
        pltpu.VMEM((4, 2, 2, SIDE, HD), BF16),
        pltpu.VMEM((4, 8, 2 * SIDE), F32),
        pltpu.VMEM((4, 8, 2 * SIDE), F32),
        pltpu.VMEM((4, HD, SIDE), F32),
        pltpu.VMEM((4, HD, SIDE), F32),
        pltpu.VMEM((4, HD, SIDE), F32),
        pltpu.VMEM((NCHUNK, 2, 4, 4, TOK, HD), BF16),
        pltpu.VMEM((NCHUNK, ROWS // 2, CHUNK), F32),
        pltpu.VMEM((NCHUNK, ROWS // 2, CHUNK), F32),
        pltpu.VMEM((NCHUNK, ROWS // 2, CHUNK), F32),
        pltpu.VMEM((NCHUNK, NZ, OWN, CHUNK), BF16),
        pltpu.VMEM((NCHUNK, NZ, OWN, CHUNK), BF16),
        dma((4,)),
        dma((4,)),
        dma((4,)),
        dma((4,)),
        dma((4,)),
        dma((4,)),
        dma((2, 4)),
        dma((2, 4)),
        dma((2, 4)),
        dma((2, 4)),
        dma((2, 4)),
        dma((2, 4)),
        dma((2, 4, 4)),
        dma((2, 4, 4)),
        dma((2, 4, 4)),
        dma((2, 4)),
        dma((NCHUNK, 2, 4)),
        dma((NCHUNK, 2, 4)),
        dma((NCHUNK, 2, 4)),
        dma((NCHUNK, 2, 4)),
        dma((2, 4)),
        dma((2, 4)),
        dma((2, 4)),
        dma((2, 4)),
        dma((NCHUNK,)),
        dma((NCHUNK,)),
        dma((NCHUNK, NZ)),
        dma((NCHUNK, NZ)),
    ]
    return pl.pallas_call(
        fused_kernel,
        name="attention_backward_and_weight_gradient",
        out_shape=jax.ShapeDtypeStruct((OWN, NCHUNK * CHUNK), F32),
        in_specs=[
            pl.BlockSpec(memory_space=pltpu.SMEM),
            pl.BlockSpec(memory_space=pl.ANY),
            vmem,
            vmem,
            vmem,
            vmem,
        ],
        out_specs=vmem,
        scratch_shapes=scratch,
        compiler_params=pltpu.CompilerParams(
            collective_id=0, has_side_effects=True, vmem_limit_bytes=60 * 2**20
        ),
    )(order, x, q, k, v, o)


def per_device(
    layer_input,
    query_rows,
    key_rows,
    value_rows,
    out_grad,
    block_order,
    master,
    moment_one,
    moment_two,
):
    grad_local = fused(
        block_order, layer_input[0], query_rows[0], key_rows[0], value_rows[0], out_grad[0]
    )
    new_one = BETA_ONE * moment_one + (1.0 - BETA_ONE) * grad_local
    new_two = BETA_TWO * moment_two + (1.0 - BETA_TWO) * grad_local * grad_local
    corr_one = 1.0 - BETA_ONE**STEP
    corr_two = 1.0 - BETA_TWO**STEP
    update = new_one / corr_one / (jnp.sqrt(new_two / corr_two) + EPSILON)
    new_master = master - LEARN_RATE * (update + DECAY * master)
    return (new_master, new_one, new_two)


def solution(mesh):
    rows = P("dp", "ctx", None)
    owned = P(("dp", "ctx"), None)
    return jax.shard_map(
        per_device,
        mesh=mesh,
        in_specs=(rows, rows, rows, rows, rows, P(), owned, owned, owned),
        out_specs=(owned, owned, owned),
        check_vma=False,
    )
```
